32 devices in a mesh: groups: 2 (over y), gx: 4 (over z), gy: 2 (over x), gz: 2 (over core).
Axes of the slice: x: 2, y: 2, z: 4, core: 2. Of those that a mesh axis runs over, the one named last changes fastest.
Arguments:
- tokens: bfloat16 [16, 8, 32, 128], P(('groups', 'gx'), 'gy', 'gz'), parts along dimension 0, may hold values from -6 to 6
- norm_gain: float32 [128], replicated, may hold values from 0.1 to 1.9
- project_weight: bfloat16 [128, 384], replicated, may hold values from -0.5 to 0.5
- output_weight: bfloat16 [128, 128], replicated, may hold values from -0.5 to 0.5
- position_bias: float32 [4, 125], replicated, may hold values from -3 to 333
- grad_output: bfloat16 [16, 8, 32, 128], P(('groups', 'gx'), 'gy', 'gz'), parts along dimension 0, may hold values from -6 to 6
Outputs:
- token_grad: float32 [16, 8, 32, 128], P(('groups', 'gx'), 'gy', 'gz'), parts along dimension 0
- project_grad: float32 [256, 384], P('groups'), parts along dimension 0
- output_grad: float32 [256, 128], P('groups'), parts along dimension 0
- gain_grad: float32 [256], P('groups'), parts along dimension 0
- bias_grad: float32 [8, 125], P('groups'), parts along dimension 0
The draws below stay inside these ranges and needn't reach their ends.
There are 2 independent parts, one for each index of `groups`. The reference program is written for one: setup_inputs(seed, part) draws one part's arguments, and reference() takes and returns one part's arrays. A program takes and returns all parts, laid end to end along the dimension named above; an argument that names none is the same for every part. Nothing has to cross between parts.
All inputs are finite; a program needn't handle non-finite values.
Results may differ from the reference program's by a relative error of at most 0.0088.
Values may be sent and summed in bfloat16 or wider, within the bound.
A program may use at most 64 MiB of HBM per device.

```python
import jax
import jax.numpy as jnp
from jax import lax

WIDTH = 128
HEADS = 4
WIN = 5
NX = 8
NY = 8
NZ = 32


def draw_position_bias(key, part):
    return jax.random.uniform(jax.random.fold_in(key, 9), (HEADS, WIN ** 3), jnp.float32, -3.0, 3.0)


def shard_levels(key, extent, cuts, least, largest):
    loudness = 1.0
    for axis_at, parts in cuts:
        heights = jax.random.uniform(jax.random.fold_in(jax.random.fold_in(key, 6), axis_at), (parts,), jnp.float32, least / len(cuts), largest / len(cuts))
        loudness = loudness * jnp.repeat(jnp.exp(heights), extent[axis_at] // parts).reshape((-1,) + (1,) * (len(extent) - 1 - axis_at))
    return loudness


def scatter_about(rng, dims, scale, most, cuts=(), kind=jnp.bfloat16):
    entries = jax.random.normal(rng, dims, jnp.float32) * scale
    if len(cuts) > 0:
        entries = shard_levels(rng, dims, cuts, -0.22, 0.18) * entries
    return jnp.clip(entries, min=-most, max=most).astype(kind)


def setup_inputs(seed: int = 0, part: int = 0) -> dict:
    key_of = jax.random.split(jax.random.key(seed), 7)
    own_keys = jax.random.split(jax.random.fold_in(key_of[6], part), 7)
    tokens = scatter_about(own_keys[0], (NX, NY, NZ, WIDTH), 1.0, 6.0, ((0, 4), (1, 2), (2, 2)))
    norm_gain = jnp.clip(1.0 + 0.18 * jax.random.normal(key_of[1], (WIDTH,), jnp.float32), 0.1, 1.9)
    project_weight = scatter_about(key_of[2], (WIDTH, 3 * WIDTH), WIDTH ** -0.5, 0.5)
    output_weight = scatter_about(key_of[3], (WIDTH, WIDTH), WIDTH ** -0.5, 0.5)
    position_bias = draw_position_bias(jax.random.fold_in(key_of[6], 71), part)
    grad_output = scatter_about(own_keys[5], (NX, NY, NZ, WIDTH), 1.0, 6.0, ((0, 4), (1, 2), (2, 2)))
    return dict(tokens=tokens, norm_gain=norm_gain, project_weight=project_weight, output_weight=output_weight, position_bias=position_bias, grad_output=grad_output)


def normalize(tokens, norm_gain):
    values = tokens.astype(jnp.float32)
    inverse = lax.rsqrt(lax.optimization_barrier(jnp.mean(values * values, axis=-1, keepdims=True)) + 1e-06)
    scaled = values * inverse
    return ((scaled * norm_gain).astype(jnp.bfloat16), scaled, inverse)

def split_offset(offset):
    return (offset // (WIN * WIN), offset // WIN % WIN, offset % WIN)

def window(source, offset):
    along_x, along_y, along_z = split_offset(offset)
    anchor = offset - offset
    starts = (along_x, along_y, along_z) + (anchor,) * (source.ndim - 3)
    return lax.dynamic_slice(source, starts, (NX, NY, NZ) + source.shape[3:])

def reference(tokens, norm_gain, project_weight, output_weight, position_bias, grad_output):
    channels = tokens.shape[-1]
    head_size = channels // HEADS
    radius = WIN // 2
    offset_count = WIN ** 3
    logit_scale = head_size ** (-0.5)
    row_count = NX * NY * NZ
    factor = row_count ** (-0.5)
    hidden, scaled, inverse = normalize(tokens, norm_gain)
    hidden_rows = hidden.reshape(row_count, channels)
    projected = jnp.dot(hidden_rows, project_weight, preferred_element_type=jnp.float32).astype(jnp.bfloat16)
    projected = projected.reshape(NX, NY, NZ, 3 * channels)
    queries = projected[..., :channels].astype(jnp.float32).reshape(NX, NY, NZ, HEADS, head_size)
    pad_spec = ((radius, radius),) * 3 + ((0, 0),)
    key_values = jnp.pad(projected[..., channels:], pad_spec).astype(jnp.float32)
    inside_grid = jnp.pad(jnp.ones((NX, NY, NZ, 1), jnp.float32), pad_spec)
    offsets = jnp.arange(offset_count, dtype=jnp.int32)

    def key_at(offset):
        return window(key_values, offset)[..., :channels].reshape(NX, NY, NZ, HEADS, head_size)

    def value_at(offset):
        return window(key_values, offset)[..., channels:].reshape(NX, NY, NZ, HEADS, head_size)

    def score_at(offset):
        bias_col = lax.dynamic_slice_in_dim(position_bias, offset, 1, 1)[:, 0]
        logits = lax.optimization_barrier(jnp.sum(queries * key_at(offset), axis=-1)) * logit_scale + bias_col
        allowed = window(inside_grid, offset)
        return (jnp.where(allowed > 0, logits, -1e+30), allowed)
    scores, allowed = lax.map(score_at, offsets)
    row_peak = lax.optimization_barrier(jnp.max(scores, axis=0))
    weights = jnp.exp(scores - row_peak) * allowed
    attn_probs = weights / lax.optimization_barrier(jnp.sum(weights, axis=0))
    probs_low = attn_probs.astype(jnp.bfloat16)
    first_index = jnp.int32(0)
    last_index = jnp.int32(offset_count)

    def add_values(offset, running):
        return running + probs_low[offset].astype(jnp.float32)[..., None] * value_at(offset)
    gathered = lax.fori_loop(first_index, last_index, add_values, jnp.zeros((NX, NY, NZ, HEADS, head_size), jnp.float32))
    attended = gathered.astype(jnp.bfloat16)
    attended_rows = attended.reshape(row_count, channels)
    grad_rows = grad_output.reshape(row_count, channels)
    output_grad = jnp.dot(attended_rows.T, grad_rows, preferred_element_type=jnp.float32) * factor
    d_attended = jnp.dot(grad_rows, output_weight.T, preferred_element_type=jnp.float32).astype(jnp.bfloat16)
    d_heads = d_attended.astype(jnp.float32).reshape(NX, NY, NZ, HEADS, head_size)
    centre = lax.optimization_barrier(jnp.sum(d_heads * attended.astype(jnp.float32), axis=-1))

    def prob_grad(offset):
        return lax.optimization_barrier(jnp.sum(d_heads * value_at(offset), axis=-1))
    d_probs = lax.map(prob_grad, offsets)
    d_scores = attn_probs * (d_probs - centre)
    bias_grad = lax.optimization_barrier(jnp.sum(d_scores, axis=(1, 2, 3))).T * factor
    d_low = (d_scores * logit_scale).astype(jnp.bfloat16)

    def add_query(offset, running):
        return running + d_low[offset].astype(jnp.float32)[..., None] * key_at(offset)
    d_query = lax.fori_loop(first_index, last_index, add_query, jnp.zeros((NX, NY, NZ, HEADS, head_size), jnp.float32))

    def add_pairs(offset, running):
        along_x, along_y, along_z = split_offset(offset)
        d_key = (d_low[offset].astype(jnp.float32)[..., None] * queries).reshape(NX, NY, NZ, channels)
        d_value = (probs_low[offset].astype(jnp.float32)[..., None] * d_heads).reshape(NX, NY, NZ, channels)
        update = jnp.concatenate([d_key, d_value], axis=-1)
        return lax.dynamic_update_slice(running, window(running, offset) + update, (along_x, along_y, along_z, offset - offset))
    pair_shape = (NX + 2 * radius, NY + 2 * radius, NZ + 2 * radius, 2 * channels)
    d_pairs = lax.fori_loop(first_index, last_index, add_pairs, jnp.zeros(pair_shape, jnp.float32))
    d_kv = d_pairs[radius:radius + NX, radius:radius + NY, radius:radius + NZ]
    d_project = jnp.concatenate([d_query.reshape(row_count, channels), d_kv.reshape(row_count, 2 * channels)], axis=1)
    project_grad = jnp.dot(hidden_rows.astype(jnp.float32).T, d_project, precision=lax.Precision.HIGHEST) * factor
    d_hidden = jnp.dot(d_project, project_weight.astype(jnp.float32).T, precision=lax.Precision.HIGHEST)
    scaled_rows = scaled.reshape(row_count, channels)
    inverse_rows = inverse.reshape(row_count, 1)
    gain_grad = lax.optimization_barrier(jnp.sum(d_hidden * scaled_rows, axis=0)) * factor
    d_scaled = d_hidden * norm_gain
    token_grad = inverse_rows * (d_scaled - scaled_rows * lax.optimization_barrier(jnp.mean(d_scaled * scaled_rows, axis=-1, keepdims=True)))
    token_grad = token_grad.reshape(NX, NY, NZ, channels)
    return (token_grad, project_grad, output_grad, gain_grad, bias_grad)
```

```python
import functools

import jax
import jax.numpy as jnp
from jax import lax
from jax.experimental import pallas as pl
from jax.experimental.pallas import tpu as pltpu
from jax.sharding import PartitionSpec as P

WIN = 5
RADIUS = 2
FAR = -1e30
BF = jnp.bfloat16
F32 = jnp.float32


def dot(a, b, over):
    return lax.dot_general(a, b, ((over[:1], over[1:]), ((), ())), preferred_element_type=F32)


def digits(index, steps):
    out = []
    for step, count in steps:
        digit = jnp.zeros_like(index)
        for i in range(1, count):
            digit = digit + (index >= step * i).astype(jnp.int32)
        index = index - digit * step
        out.append(digit)
    return out


def one_hot(dims, lanes):
    _, pad_y, pad_z = dims
    rows = lax.broadcasted_iota(jnp.int32, (128, 1), 0)
    i, j, l = digits(rows, ((WIN * WIN, WIN + 1), (WIN, WIN), (1, WIN)))
    code = jnp.where(rows < WIN**3, (i * pad_y + j) * pad_z + l, -1)
    return (lax.broadcasted_iota(jnp.int32, (128, lanes), 1) == code).astype(F32)


def bias_table(bias_ref, spread, table, inner, dims, lanes, extents):
    heads = bias_ref.shape[0]
    size_x, size_y, size_z = inner
    pad_x, pad_y, pad_z = dims
    spread[...] = jnp.zeros_like(spread)
    spread[0:heads, 0 : WIN**3] = bias_ref[...]
    base = lax.dot_general(
        spread[...],
        one_hot(dims, lanes),
        (((1,), (0,)), ((), ())),
        precision=lax.Precision.HIGHEST,
        preferred_element_type=F32,
    )
    lane = lax.broadcasted_iota(jnp.int32, (1, lanes), 1)
    at = digits(lane, ((pad_y * pad_z, pad_x + 2), (pad_z, pad_y), (1, pad_z)))
    near = (at[0] < WIN) & (at[1] < WIN) & (at[2] < WIN)
    base = jnp.where(near, base, FAR)
    valid = lane < pad_x * pad_y * pad_z
    for digit, size, (place, extent) in zip(at, inner, extents):
        position = digit + (place * size - RADIUS)
        valid = valid & (position >= 0) & (position < extent)
    row = lax.broadcasted_iota(jnp.int32, (size_z, 1), 0)
    for h in range(heads):
        turned = jnp.broadcast_to(base[h : h + 1], (size_z, lanes))
        bit = 1
        while bit < size_z:
            turned = jnp.where((row & bit) > 0, pltpu.roll(turned, bit, 1), turned)
            bit *= 2
        for x in range(size_x):
            for y in range(size_y):
                shift = (x * pad_y + y) * pad_z
                moved = pltpu.roll(turned, shift, 1) if shift else turned
                at_row = ((h * size_x + x) * size_y + y) * size_z
                table[at_row : at_row + size_z, :] = jnp.where(valid, moved, FAR)


def bias_fold(d_scores, inner, dims, lanes):
    size_x, size_y, size_z = inner
    _, pad_y, pad_z = dims
    total = None
    for x in range(size_x):
        for y in range(size_y):
            at_row = (x * size_y + y) * size_z
            shift = (x * pad_y + y) * pad_z
            part = d_scores[at_row : at_row + size_z, :]
            part = pltpu.roll(part, lanes - shift, 1) if shift else part
            total = part if total is None else total + part
    rows = size_z
    while rows > 8:
        rows //= 2
        total = total[:rows] + pltpu.roll(total[rows:], lanes - rows, 1)
    step = rows // 2
    while step >= 1:
        moved = pltpu.roll(total, lanes - step, 1)
        total = total + pltpu.roll(moved, rows - step, 0)
        step //= 2
    return total[0:1]


def normed(x, gain):
    inverse = lax.rsqrt(jnp.mean(x * x, axis=-1, keepdims=True) + 1e-06)
    scaled = x * inverse
    return (scaled * gain).astype(BF), scaled, inverse


def attention_grads(
    padded, local, gain, project_ref, output_ref, go, table, probs_s, low_s, inner, dims, heads
):
    lanes, channels = padded.shape
    rows = local.shape[0]
    head = channels // heads
    scale = head ** (-0.5)
    hidden, scaled, _ = normed(padded, gain)
    hidden_l, scaled_l, inverse_l = normed(local, gain)
    keys = jnp.dot(hidden, project_ref[:, channels : 2 * channels], preferred_element_type=F32).astype(BF)
    values = jnp.dot(hidden, project_ref[:, 2 * channels :], preferred_element_type=F32).astype(BF)
    queries = jnp.dot(hidden_l, project_ref[:, :channels], preferred_element_type=F32).astype(BF)
    d_att = dot(go, output_ref[...], (1, 1)).astype(BF)
    column = lax.broadcasted_iota(jnp.int32, (1, channels), 1)
    attended = jnp.zeros((rows, channels), F32)
    d_query = jnp.zeros((rows, channels), F32)
    query_parts, grad_parts, bias_parts = [], [], []
    for h in range(heads):
        mine = (column >= h * head) & (column < (h + 1) * head)
        q = jnp.where(mine, queries.astype(F32), 0.0).astype(BF)
        da = jnp.where(mine, d_att.astype(F32), 0.0).astype(BF)
        query_parts.append(q)
        grad_parts.append(da)
        span = slice(h * rows, (h + 1) * rows)
        scores = dot(q, keys, (1, 1)) * scale + table[span, :]
        weights = jnp.exp(scores - jnp.max(scores, axis=1, keepdims=True))
        probs = weights * (1.0 / jnp.sum(weights, axis=1, keepdims=True))
        probs_low = probs.astype(BF)
        probs_s[span, :] = probs_low
        gathered = jnp.dot(probs_low, values, preferred_element_type=F32)
        gathered = jnp.where(mine, gathered, 0.0).astype(BF).astype(F32)
        attended = attended + gathered
        centre = jnp.sum(da.astype(F32) * gathered, axis=1, keepdims=True)
        d_scores = probs * (dot(da, values, (1, 1)) - centre)
        bias_parts.append(bias_fold(d_scores, inner, dims, lanes))
        low = (d_scores * scale).astype(BF)
        low_s[span, :] = low
        d_query = d_query + jnp.where(mine, jnp.dot(low, keys, preferred_element_type=F32), 0.0)
    attended = attended.astype(BF)
    d_keys = dot(low_s[...], jnp.concatenate(query_parts, axis=0), (0, 0)).astype(BF)
    d_values = dot(probs_s[...], jnp.concatenate(grad_parts, axis=0), (0, 0)).astype(BF)
    d_query = d_query.astype(BF)
    d_hidden = dot(d_keys, project_ref[:, channels : 2 * channels], (1, 1)) + dot(
        d_values, project_ref[:, 2 * channels :], (1, 1)
    )
    d_hidden_l = dot(d_query, project_ref[:, :channels], (1, 1))
    project = (
        dot(hidden_l, d_query, (0, 0)),
        dot(hidden, d_keys, (0, 0)),
        dot(hidden, d_values, (0, 0)),
    )
    output = dot(attended, go, (0, 0))
    gain_sum = jnp.sum(d_hidden * scaled, axis=0, keepdims=True) + jnp.sum(
        d_hidden_l * scaled_l, axis=0, keepdims=True
    )
    folded = jnp.concatenate(bias_parts + [jnp.zeros((8 - heads, lanes), F32)], axis=0)
    bias_sum = lax.dot_general(
        folded,
        one_hot(dims, lanes),
        (((1,), (1,)), ((), ())),
        precision=lax.Precision.HIGHEST,
        preferred_element_type=F32,
    )
    return d_hidden, d_hidden_l, project, output, gain_sum, bias_sum, scaled_l, inverse_l


def kernel(
    inner, dims, sizes, padded_ref, local_ref, gain_ref, project_ref, output_ref, bias_ref, go_ref,
    dh_ref, dhl_ref, sums_ref, table, probs_s, low_s, spread,
):
    lanes, channels = padded_ref.shape
    extents = [
        (lax.axis_index(axis), size * cells)
        for axis, size, cells in zip(("gx", "gy", "gz"), sizes, inner)
    ]
    bias_table(bias_ref, spread, table, inner, dims, lanes, extents)
    d_hidden, d_hidden_l, project, output, gain_sum, bias_sum, _, _ = attention_grads(
        padded_ref[...], local_ref[...].astype(F32), gain_ref[...], project_ref, output_ref,
        go_ref[...], table, probs_s, low_s, inner, dims, bias_ref.shape[0],
    )
    dh_ref[...] = d_hidden
    dhl_ref[...] = d_hidden_l
    for i in range(3):
        sums_ref[i * channels : (i + 1) * channels, :] = project[i]
    sums_ref[3 * channels : 4 * channels, :] = output
    sums_ref[4 * channels : 4 * channels + 8, :] = bias_sum
    sums_ref[4 * channels + 8 : 4 * channels + 16, :] = jnp.broadcast_to(gain_sum, (8, channels))


def with_halo(array, sides, width):
    for axis, dim in sides:
        size, length = (lax.axis_size(axis), array.shape[dim])
        up = [(i, i + 1) for i in range(size - 1)]
        down = [(j, i) for i, j in up]
        last = lax.slice_in_dim(array, length - width, length, axis=dim)
        leading = lax.slice_in_dim(array, 0, width, axis=dim)
        before = lax.ppermute(last, axis, up)
        after = lax.ppermute(leading, axis, down)
        array = jnp.concatenate([before, array, after], axis=dim)
    return array


def fold_halo(array, sides, width):
    for axis, dim in sides:
        size, length = (lax.axis_size(axis), array.shape[dim])
        up = [(i, i + 1) for i in range(size - 1)]
        down = [(j, i) for i, j in up]
        low = lax.ppermute(lax.slice_in_dim(array, 0, width, axis=dim), axis, down)
        high = lax.ppermute(lax.slice_in_dim(array, length - width, length, axis=dim), axis, up)
        array = lax.slice_in_dim(array, width, length - width, axis=dim)
        inner = length - 2 * width
        pads = [[(0, 0)] * array.ndim for _ in range(2)]
        pads[0][dim] = (inner - width, 0)
        pads[1][dim] = (0, inner - width)
        array = array + jnp.pad(low, pads[0]) + jnp.pad(high, pads[1])
    return array


def shards(tokens, norm_gain, project_weight, output_weight, position_bias, grad_output):
    inner, channels = tokens.shape[:3], tokens.shape[3]
    heads = position_bias.shape[0]
    sizes = tuple(lax.axis_size(axis) for axis in ("gx", "gy", "gz"))
    dims = tuple(size + 2 * RADIUS for size in inner)
    rows = inner[0] * inner[1] * inner[2]
    count = dims[0] * dims[1] * dims[2]
    lanes = -(-count // 128) * 128
    factor = (rows * sizes[0] * sizes[1] * sizes[2]) ** (-0.5)
    padded = with_halo(tokens, (("gx", 0), ("gy", 1), ("gz", 2)), RADIUS)
    padded = jnp.pad(padded.astype(F32).reshape(count, channels), ((0, lanes - count), (0, 0)))
    d_hidden, d_hidden_l, sums = pl.pallas_call(
        functools.partial(kernel, inner, dims, sizes),
        out_shape=(
            jax.ShapeDtypeStruct((lanes, channels), F32),
            jax.ShapeDtypeStruct((rows, channels), F32),
            jax.ShapeDtypeStruct((4 * channels + 16, channels), F32),
        ),
        in_specs=[pl.BlockSpec(memory_space=pltpu.VMEM)] * 7,
        out_specs=(pl.BlockSpec(memory_space=pltpu.VMEM),) * 3,
        scratch_shapes=[
            pltpu.VMEM((heads * rows, lanes), F32),
            pltpu.VMEM((heads * rows, lanes), BF),
            pltpu.VMEM((heads * rows, lanes), BF),
            pltpu.VMEM((8, 128), F32),
        ],
        compiler_params=pltpu.CompilerParams(vmem_limit_bytes=40 * 2**20),
    )(
        padded,
        tokens.reshape(rows, channels),
        norm_gain.reshape(1, channels),
        project_weight,
        output_weight,
        position_bias,
        grad_output.reshape(rows, channels),
    )
    summed = lax.psum(sums, ("gx", "gy", "gz")) * factor
    grid = d_hidden[:count].reshape(dims + (channels,))
    mine = fold_halo(grid, (("gz", 2), ("gy", 1), ("gx", 0)), RADIUS).reshape(rows, channels)
    d_scaled = (mine + d_hidden_l) * norm_gain
    x = tokens.reshape(rows, channels).astype(F32)
    inverse = lax.rsqrt(jnp.mean(x * x, axis=-1, keepdims=True) + 1e-06)
    scaled = x * inverse
    token_grad = inverse * (d_scaled - scaled * jnp.mean(d_scaled * scaled, axis=-1, keepdims=True))
    project_grad = jnp.concatenate(
        [summed[i * channels : (i + 1) * channels] for i in range(3)], axis=1
    )
    return (
        token_grad.reshape(tokens.shape),
        project_grad,
        summed[3 * channels : 4 * channels],
        summed[4 * channels + 8],
        summed[4 * channels : 4 * channels + heads, : WIN**3],
    )


def solution(mesh):
    tokens = P(("groups", "gx"), "gy", "gz", None)
    return jax.shard_map(
        shards,
        mesh=mesh,
        in_specs=(tokens, P(), P(), P(), P(), tokens),
        out_specs=(tokens, P("groups", None), P("groups", None), P("groups"), P("groups", None)),
        check_vma=False,
    )
```

```python
import functools

import jax
import jax.numpy as jnp
from jax import lax
from jax.experimental import pallas as pl
from jax.experimental.pallas import tpu as pltpu
from jax.sharding import PartitionSpec as P

WIN = 5
RADIUS = 2
FAR = -1e30
BF = jnp.bfloat16
F32 = jnp.float32


def dot(a, b, over):
    return lax.dot_general(a, b, ((over[:1], over[1:]), ((), ())), preferred_element_type=F32)


def digits(index, steps):
    out = []
    for step, count in steps:
        digit = jnp.zeros_like(index)
        for i in range(1, count):
            digit = digit + (index >= step * i).astype(jnp.int32)
        index = index - digit * step
        out.append(digit)
    return out


def one_hot(dims, lanes):
    _, pad_y, pad_z = dims
    rows = lax.broadcasted_iota(jnp.int32, (128, 1), 0)
    i, j, l = digits(rows, ((WIN * WIN, WIN + 1), (WIN, WIN), (1, WIN)))
    code = jnp.where(rows < WIN**3, (i * pad_y + j) * pad_z + l, -1)
    return (lax.broadcasted_iota(jnp.int32, (128, lanes), 1) == code).astype(F32)


def bias_table(bias_ref, spread, table, inner, dims, lanes, extents):
    heads = bias_ref.shape[0]
    size_x, size_y, size_z = inner
    pad_x, pad_y, pad_z = dims
    spread[...] = jnp.zeros_like(spread)
    spread[0:heads, 0 : WIN**3] = bias_ref[...]
    base = lax.dot_general(
        spread[...],
        one_hot(dims, lanes),
        (((1,), (0,)), ((), ())),
        precision=lax.Precision.HIGHEST,
        preferred_element_type=F32,
    )
    lane = lax.broadcasted_iota(jnp.int32, (1, lanes), 1)
    at = digits(lane, ((pad_y * pad_z, pad_x + 2), (pad_z, pad_y), (1, pad_z)))
    near = (at[0] < WIN) & (at[1] < WIN) & (at[2] < WIN)
    base = jnp.where(near, base, FAR)
    valid = lane < pad_x * pad_y * pad_z
    for digit, size, (place, extent) in zip(at, inner, extents):
        position = digit + (place * size - RADIUS)
        valid = valid & (position >= 0) & (position < extent)
    row = lax.broadcasted_iota(jnp.int32, (size_z, 1), 0)
    for h in range(heads):
        turned = jnp.broadcast_to(base[h : h + 1], (size_z, lanes))
        bit = 1
        while bit < size_z:
            turned = jnp.where((row & bit) > 0, pltpu.roll(turned, bit, 1), turned)
            bit *= 2
        for x in range(size_x):
            for y in range(size_y):
                shift = (x * pad_y + y) * pad_z
                moved = pltpu.roll(turned, shift, 1) if shift else turned
                at_row = ((h * size_x + x) * size_y + y) * size_z
                table[at_row : at_row + size_z, :] = jnp.where(valid, moved, FAR)


def bias_fold(d_scores, inner, dims, lanes):
    size_x, size_y, size_z = inner
    _, pad_y, pad_z = dims
    total = None
    for x in range(size_x):
        for y in range(size_y):
            at_row = (x * size_y + y) * size_z
            shift = (x * pad_y + y) * pad_z
            part = d_scores[at_row : at_row + size_z, :]
            part = pltpu.roll(part, lanes - shift, 1) if shift else part
            total = part if total is None else total + part
    rows = size_z
    while rows > 8:
        rows //= 2
        total = total[:rows] + pltpu.roll(total[rows:], lanes - rows, 1)
    step = rows // 2
    while step >= 1:
        moved = pltpu.roll(total, lanes - step, 1)
        total = total + pltpu.roll(moved, rows - step, 0)
        step //= 2
    return total[0:1]


def normed(x, gain):
    inverse = lax.rsqrt(jnp.mean(x * x, axis=-1, keepdims=True) + 1e-06)
    scaled = x * inverse
    return (scaled * gain).astype(BF), scaled, inverse


def attention_grads(
    padded, local, gain, project_ref, output_ref, go, table, probs_s, low_s, inner, dims, heads, send_hidden
):
    lanes, channels = padded.shape
    rows = local.shape[0]
    head = channels // heads
    scale = head ** (-0.5)
    hidden, scaled, _ = normed(padded, gain)
    hidden_l, scaled_l, inverse_l = normed(local, gain)
    keys = jnp.dot(hidden, project_ref[:, channels : 2 * channels], preferred_element_type=F32).astype(BF)
    values = jnp.dot(hidden, project_ref[:, 2 * channels :], preferred_element_type=F32).astype(BF)
    queries = jnp.dot(hidden_l, project_ref[:, :channels], preferred_element_type=F32).astype(BF)
    d_att = dot(go, output_ref[...], (1, 1)).astype(BF)
    column = lax.broadcasted_iota(jnp.int32, (1, channels), 1)
    attended = jnp.zeros((rows, channels), F32)
    d_query = jnp.zeros((rows, channels), F32)
    query_parts, grad_parts, bias_parts = [], [], []
    for h in range(heads):
        mine = (column >= h * head) & (column < (h + 1) * head)
        q = jnp.where(mine, queries.astype(F32), 0.0).astype(BF)
        da = jnp.where(mine, d_att.astype(F32), 0.0).astype(BF)
        query_parts.append(q)
        grad_parts.append(da)
        span = slice(h * rows, (h + 1) * rows)
        scores = dot(q, keys, (1, 1)) * scale + table[span, :]
        weights = jnp.exp(scores - jnp.max(scores, axis=1, keepdims=True))
        probs = weights * (1.0 / jnp.sum(weights, axis=1, keepdims=True))
        probs_low = probs.astype(BF)
        probs_s[span, :] = probs_low
        gathered = jnp.dot(probs_low, values, preferred_element_type=F32)
        gathered = jnp.where(mine, gathered, 0.0).astype(BF).astype(F32)
        attended = attended + gathered
        centre = jnp.sum(da.astype(F32) * gathered, axis=1, keepdims=True)
        d_scores = probs * (dot(da, values, (1, 1)) - centre)
        bias_parts.append(bias_fold(d_scores, inner, dims, lanes))
        low = (d_scores * scale).astype(BF)
        low_s[span, :] = low
        d_query = d_query + jnp.where(mine, jnp.dot(low, keys, preferred_element_type=F32), 0.0)
    attended = attended.astype(BF)
    d_keys = dot(low_s[...], jnp.concatenate(query_parts, axis=0), (0, 0)).astype(BF)
    d_values = dot(probs_s[...], jnp.concatenate(grad_parts, axis=0), (0, 0)).astype(BF)
    d_query = d_query.astype(BF)
    d_hidden = dot(d_keys, project_ref[:, channels : 2 * channels], (1, 1)) + dot(
        d_values, project_ref[:, 2 * channels :], (1, 1)
    )
    send_hidden(d_hidden)
    d_hidden_l = dot(d_query, project_ref[:, :channels], (1, 1))
    project = (
        dot(hidden_l, d_query, (0, 0)),
        dot(hidden, d_keys, (0, 0)),
        dot(hidden, d_values, (0, 0)),
    )
    output = dot(attended, go, (0, 0))
    gain_sum = jnp.sum(d_hidden * scaled, axis=0, keepdims=True) + jnp.sum(
        d_hidden_l * scaled_l, axis=0, keepdims=True
    )
    folded = jnp.concatenate(bias_parts + [jnp.zeros((8 - heads, lanes), F32)], axis=0)
    bias_sum = lax.dot_general(
        folded,
        one_hot(dims, lanes),
        (((1,), (1,)), ((), ())),
        precision=lax.Precision.HIGHEST,
        preferred_element_type=F32,
    )
    return d_hidden, d_hidden_l, project, output, gain_sum, bias_sum, scaled_l, inverse_l


MESH = pl.DeviceIdType.MESH
AXES = ("gx", "gy", "gz")
TURNS = [(x, y, z) for x in (0, -1, 1) for y in (0, -1, 1) for z in (0, -1, 1)][1:]
FLAT = [turn for turn in TURNS if turn[2] == 0]
EDGES = [turn for turn in TURNS if turn[2] != 0]


def span_of(turn, size):
    return {0: (0, size), 1: (size - RADIUS, size), -1: (0, RADIUS)}[turn]


def rim_of(turn, size):
    return {
        0: (RADIUS, size + RADIUS),
        1: (size + RADIUS, size + 2 * RADIUS),
        -1: (0, RADIUS),
    }[turn]


def kernel(
    inner, dims, sizes, factor, chunk,
    tokens_ref, gain_ref, project_ref, output_ref, bias_ref, go_ref,
    token_out, project_out, output_out, gain_out, bias_out,
    table, probs_s, low_s, spread,
    edge_f, edge, main, rims, padded, hidden_f, pack_f, out_main, out_edge, in_main, in_edge,
    sums_f, sums, parts, final,
    tok_send, tok_recv, ret_send, ret_recv, rs_send, rs_recv, ag_send, ag_recv,
):
    size_x, size_y, size_z = inner
    pad_x, pad_y, pad_z = dims
    rows = size_x * size_y * size_z
    lanes, channels = padded.shape
    heads = bias_ref.shape[0]
    here = [lax.axis_index(axis) for axis in AXES]
    count = sizes[0] * sizes[1] * sizes[2]
    me = (here[0] * sizes[1] + here[1]) * sizes[2] + here[2]

    def peer(k):
        other = lax.rem(me + k, count)
        rest = lax.div(other, sizes[2])
        place = (lax.div(rest, sizes[1]), lax.rem(rest, sizes[1]), lax.rem(other, sizes[2]))
        return other, dict(zip(AXES, place))

    def exists(turn, sign):
        ok = None
        for at, size, step in zip(here, sizes, turn):
            if step:
                this = (at + sign * step >= 0) & (at + sign * step < size)
                ok = this if ok is None else ok & this
        return ok

    def neighbour(turn):
        return {axis: at + step for axis, at, step in zip(AXES, here, turn)}

    main[...] = jnp.zeros_like(main)
    rims[...] = jnp.zeros_like(rims)
    in_main[...] = jnp.zeros_like(in_main)
    in_edge[...] = jnp.zeros_like(in_edge)
    barrier = pltpu.get_barrier_semaphore()

    def greet(k, carry):
        pl.semaphore_signal(barrier, inc=1, device_id=peer(k)[1], device_id_type=MESH)
        return carry

    lax.fori_loop(1, count, greet, 0)
    for x in range(size_x):
        for y in range(size_y):
            line = tokens_ref[x, y].astype(F32)
            at = (x * size_y + y) * RADIUS
            edge_f[0, at : at + RADIUS, :] = line[:RADIUS]
            edge_f[1, at : at + RADIUS, :] = line[size_z - RADIUS :]
    edge[...] = edge_f[...].astype(BF)
    pl.semaphore_wait(barrier, count - 1)

    def token_copy(turn):
        n = TURNS.index(turn)
        if turn[2]:
            source = edge.at[1 if turn[2] > 0 else 0]
            target = rims.at[EDGES.index(turn)]
        else:
            (x0, x1), (y0, y1) = (span_of(t, s) for t, s in zip(turn[:2], inner[:2]))
            (u0, u1), (v0, v1) = (rim_of(-t, s) for t, s in zip(turn[:2], inner[:2]))
            source = tokens_ref.at[x0:x1, y0:y1]
            target = main.at[u0:u1, v0:v1]
        return pltpu.make_async_remote_copy(
            src_ref=source, dst_ref=target, send_sem=tok_send.at[n], recv_sem=tok_recv.at[n],
            device_id=neighbour(turn), device_id_type=MESH,
        )

    def grad_copy(turn):
        n = TURNS.index(turn)
        if turn[2]:
            source, target = (buffer.at[EDGES.index(turn)] for buffer in (out_edge, in_edge))
        else:
            (u0, u1), (v0, v1) = (rim_of(t, s) for t, s in zip(turn[:2], inner[:2]))
            source = out_main.at[u0:u1, v0:v1]
            target = in_main.at[FLAT.index(turn), 0 : u1 - u0, 0 : v1 - v0]
        return pltpu.make_async_remote_copy(
            src_ref=source, dst_ref=target, send_sem=ret_send.at[n], recv_sem=ret_recv.at[n],
            device_id=neighbour(turn), device_id_type=MESH,
        )

    def every(make, sign, what):
        for turn in TURNS:
            pl.when(exists(turn, sign))(lambda turn=turn: getattr(make(turn), what)())

    every(token_copy, 1, "start")
    bias_table(
        bias_ref, spread, table, inner, dims, lanes,
        [(at, size * cells) for at, size, cells in zip(here, sizes, inner)],
    )
    every(token_copy, -1, "wait_recv")

    filled = pad_x * pad_y * pad_z
    if filled < lanes:
        padded[filled:, :] = jnp.zeros((lanes - filled, channels), F32)
    sides = [
        [(t, u - rim_of(-t, s)[0] + span_of(t, s)[0]) for u in range(s + 2 * RADIUS)
         for t in (0, 1, -1) if rim_of(-t, s)[0] <= u < rim_of(-t, s)[1]]
        for s in inner[:2]
    ]
    for u in range(pad_x):
        for v in range(pad_y):
            (turn_x, x), (turn_y, y) = sides[0][u], sides[1][v]
            at = (u * pad_y + v) * pad_z
            own = turn_x == 0 and turn_y == 0
            line = tokens_ref[x, y] if own else main[u, v]
            padded[at + RADIUS : at + RADIUS + size_z, :] = line.astype(F32)
            row = (x * size_y + y) * RADIUS
            for turn_z, to in ((1, at), (-1, at + RADIUS + size_z)):
                tile = rims[EDGES.index((turn_x, turn_y, turn_z))].astype(F32)
                padded[to : to + RADIUS, :] = tile[row : row + RADIUS]

    def send_hidden(d_hidden):
        hidden_f[...] = d_hidden
        pack_f[...] = jnp.zeros_like(pack_f)
        for u in range(pad_x):
            for v in range(pad_y):
                (turn_x, x), (turn_y, y) = sides[0][u], sides[1][v]
                at = (u * pad_y + v) * pad_z
                out_main[u, v] = hidden_f[at + RADIUS : at + RADIUS + size_z, :].astype(BF)
                row = (x * size_y + y) * RADIUS
                for turn_z, to in ((-1, at), (1, at + RADIUS + size_z)):
                    slot = EDGES.index((-turn_x, -turn_y, turn_z))
                    pack_f[slot, row : row + RADIUS, :] = hidden_f[to : to + RADIUS, :]
        out_edge[...] = pack_f[...].astype(BF)
        every(grad_copy, 1, "start")

    _, d_hidden_l, project, output, gain_sum, bias_sum, scaled, inverse = attention_grads(
        padded[...], tokens_ref[...].astype(F32).reshape(rows, channels), gain_ref[...],
        project_ref, output_ref, go_ref[...], table, probs_s, low_s, inner, dims, heads,
        send_hidden,
    )
    used = 4 * channels
    for i in range(3):
        sums_f[i * channels : (i + 1) * channels, :] = project[i]
    sums_f[3 * channels : used, :] = output
    sums_f[used : used + 8, :] = bias_sum
    sums_f[used + 8 : used + 16, :] = jnp.broadcast_to(gain_sum, (8, channels))
    if count * chunk > used + 16:
        sums_f[used + 16 :, :] = jnp.zeros((count * chunk - used - 16, channels), F32)
    sums[...] = sums_f[...].astype(BF).reshape(count, chunk, channels)

    def part_copy(k):
        other, place = peer(k)
        return pltpu.make_async_remote_copy(
            src_ref=sums.at[other], dst_ref=parts.at[k], send_sem=rs_send.at[k],
            recv_sem=rs_recv.at[k], device_id=place, device_id_type=MESH,
        )

    def whole_copy(k):
        place = peer(k)[1]
        return pltpu.make_async_remote_copy(
            src_ref=final.at[me], dst_ref=final.at[me], send_sem=ag_send.at[k],
            recv_sem=ag_recv.at[k], device_id=place, device_id_type=MESH,
        )

    def whole_arrival(k):
        other = lax.rem(me + count - k, count)
        return pltpu.make_async_remote_copy(
            src_ref=final.at[other], dst_ref=final.at[other], send_sem=ag_send.at[k],
            recv_sem=ag_recv.at[k], device_id=peer(k)[1], device_id_type=MESH,
        )

    def loop(body):
        lax.fori_loop(1, count, lambda k, carry: (body(k), carry)[1], 0)

    loop(lambda k: part_copy(k).start())

    every(grad_copy, -1, "wait_recv")
    norm_scaled = d_hidden_l
    low = jnp.zeros(in_edge.shape[1:], F32)
    high = jnp.zeros(in_edge.shape[1:], F32)
    for n, turn in enumerate(EDGES):
        if turn[2] > 0:
            low = low + in_edge[n].astype(F32)
        else:
            high = high + in_edge[n].astype(F32)
    for x in range(size_x):
        for y in range(size_y):
            at = ((x + RADIUS) * pad_y + y + RADIUS) * pad_z + RADIUS
            line = hidden_f[at : at + size_z, :]
            for n, (turn_x, turn_y, _) in enumerate(FLAT):
                (x0, x1), (y0, y1) = span_of(-turn_x, size_x), span_of(-turn_y, size_y)
                if x0 <= x < x1 and y0 <= y < y1:
                    line = line + in_main[n, x - x0, y - y0].astype(F32)
            to = (x * size_y + y) * size_z
            row = (x * size_y + y) * RADIUS
            padded[to : to + size_z, :] = line
            padded[to : to + RADIUS, :] += low[row : row + RADIUS]
            padded[to + size_z - RADIUS : to + size_z, :] += high[row : row + RADIUS]
    d_scaled = (padded[0:rows, :] + norm_scaled) * gain_ref[...]
    token_grad = inverse * (
        d_scaled - scaled * jnp.mean(d_scaled * scaled, axis=-1, keepdims=True)
    )
    token_out[...] = token_grad.reshape(inner + (channels,))

    loop(lambda k: part_copy(k).wait_recv())
    total = lax.fori_loop(
        1, count, lambda k, carry: carry + parts[k].astype(F32), sums[me].astype(F32)
    )
    final[me] = (total * factor).astype(BF)
    loop(lambda k: whole_copy(k).start())
    loop(lambda k: whole_arrival(k).wait_recv())
    done = final[...].astype(F32).reshape(count * chunk, channels)
    for i in range(3):
        project_out[:, i * channels : (i + 1) * channels] = done[i * channels : (i + 1) * channels]
    output_out[...] = done[3 * channels : used]
    bias_out[...] = done[used : used + heads, : WIN**3]
    gain_out[...] = done[used + 8 : used + 9]
    every(token_copy, 1, "wait_send")
    every(grad_copy, 1, "wait_send")
    loop(lambda k: part_copy(k).wait_send())
    loop(lambda k: whole_copy(k).wait_send())


def shards(tokens, norm_gain, project_weight, output_weight, position_bias, grad_output):
    inner, channels = tokens.shape[:3], tokens.shape[3]
    heads = position_bias.shape[0]
    sizes = tuple(lax.axis_size(axis) for axis in AXES)
    dims = tuple(size + 2 * RADIUS for size in inner)
    rows = inner[0] * inner[1] * inner[2]
    lanes = -(-dims[0] * dims[1] * dims[2] // 128) * 128
    count = sizes[0] * sizes[1] * sizes[2]
    factor = (rows * count) ** (-0.5)
    chunk = -(-(4 * channels + 16) // (16 * count)) * 16
    tile = inner[0] * inner[1] * RADIUS
    vmem = pl.BlockSpec(memory_space=pltpu.VMEM)
    many = len(TURNS)
    out = pl.pallas_call(
        functools.partial(kernel, inner, dims, sizes, factor, chunk),
        out_shape=(
            jax.ShapeDtypeStruct(tokens.shape, F32),
            jax.ShapeDtypeStruct((channels, 3 * channels), F32),
            jax.ShapeDtypeStruct((channels, channels), F32),
            jax.ShapeDtypeStruct((1, channels), F32),
            jax.ShapeDtypeStruct(position_bias.shape, F32),
        ),
        in_specs=[vmem] * 6,
        out_specs=(vmem,) * 5,
        scratch_shapes=[
            pltpu.VMEM((heads * rows, lanes), F32),
            pltpu.VMEM((heads * rows, lanes), BF),
            pltpu.VMEM((heads * rows, lanes), BF),
            pltpu.VMEM((8, 128), F32),
            pltpu.VMEM((2, tile, channels), F32),
            pltpu.VMEM((2, tile, channels), BF),
            pltpu.VMEM((dims[0], dims[1], inner[2], channels), BF),
            pltpu.VMEM((len(EDGES), tile, channels), BF),
            pltpu.VMEM((lanes, channels), F32),
            pltpu.VMEM((lanes, channels), F32),
            pltpu.VMEM((len(EDGES), tile, channels), F32),
            pltpu.VMEM((dims[0], dims[1], inner[2], channels), BF),
            pltpu.VMEM((len(EDGES), tile, channels), BF),
            pltpu.VMEM((len(FLAT),) + inner + (channels,), BF),
            pltpu.VMEM((len(EDGES), tile, channels), BF),
            pltpu.VMEM((count * chunk, channels), F32),
            pltpu.VMEM((count, chunk, channels), BF),
            pltpu.VMEM((count, chunk, channels), BF),
            pltpu.VMEM((count, chunk, channels), BF),
        ]
        + [pltpu.SemaphoreType.DMA((many,))] * 4
        + [pltpu.SemaphoreType.DMA((count,))] * 4,
        compiler_params=pltpu.CompilerParams(
            vmem_limit_bytes=40 * 2**20, collective_id=0, has_side_effects=True
        ),
    )(
        tokens,
        norm_gain.reshape(1, channels),
        project_weight,
        output_weight,
        position_bias,
        grad_output.reshape(rows, channels),
    )
    token_grad, project_grad, output_grad, gain_grad, bias_grad = out
    return token_grad, project_grad, output_grad, gain_grad.reshape(channels), bias_grad


def solution(mesh):
    tokens = P(("groups", "gx"), "gy", "gz", None)
    return jax.shard_map(
        shards,
        mesh=mesh,
        in_specs=(tokens, P(), P(), P(), P(), tokens),
        out_specs=(tokens, P("groups", None), P("groups", None), P("groups"), P("groups", None)),
        check_vma=False,
    )
```

```python
import functools

import jax
import jax.numpy as jnp
from jax import lax
from jax.experimental import pallas as pl
from jax.experimental.pallas import tpu as pltpu
from jax.sharding import PartitionSpec as P

WIN = 5
RADIUS = 2
FAR = -1e30
BF = jnp.bfloat16
F32 = jnp.float32


def dot(a, b, over):
    return lax.dot_general(a, b, ((over[:1], over[1:]), ((), ())), preferred_element_type=F32)


def digits(index, steps):
    out = []
    for step, count in steps:
        digit = jnp.zeros_like(index)
        for i in range(1, count):
            digit = digit + (index >= step * i).astype(jnp.int32)
        index = index - digit * step
        out.append(digit)
    return out


def one_hot(dims, lanes):
    _, pad_y, pad_z = dims
    rows = lax.broadcasted_iota(jnp.int32, (128, 1), 0)
    i, j, l = digits(rows, ((WIN * WIN, WIN + 1), (WIN, WIN), (1, WIN)))
    code = jnp.where(rows < WIN**3, (i * pad_y + j) * pad_z + l, -1)
    return (lax.broadcasted_iota(jnp.int32, (128, lanes), 1) == code).astype(F32)


def bias_table(bias_ref, spread, table, inner, dims, lanes, extents):
    heads = bias_ref.shape[0]
    size_x, size_y, size_z = inner
    pad_x, pad_y, pad_z = dims
    spread[...] = jnp.zeros_like(spread)
    spread[0:heads, 0 : WIN**3] = bias_ref[...]
    base = lax.dot_general(
        spread[...],
        one_hot(dims, lanes),
        (((1,), (0,)), ((), ())),
        precision=lax.Precision.HIGHEST,
        preferred_element_type=F32,
    )
    lane = lax.broadcasted_iota(jnp.int32, (1, lanes), 1)
    at = digits(lane, ((pad_y * pad_z, pad_x + 2), (pad_z, pad_y), (1, pad_z)))
    near = (at[0] < WIN) & (at[1] < WIN) & (at[2] < WIN)
    base = jnp.where(near, base, FAR)
    valid = lane < pad_x * pad_y * pad_z
    for digit, size, (place, extent) in zip(at, inner, extents):
        position = digit + (place * size - RADIUS)
        valid = valid & (position >= 0) & (position < extent)
    row = lax.broadcasted_iota(jnp.int32, (size_z, 1), 0)
    for h in range(heads):
        turned = jnp.broadcast_to(base[h : h + 1], (size_z, lanes))
        bit = 1
        while bit < size_z:
            turned = jnp.where((row & bit) > 0, pltpu.roll(turned, bit, 1), turned)
            bit *= 2
        for x in range(size_x):
            for y in range(size_y):
                shift = (x * pad_y + y) * pad_z
                moved = pltpu.roll(turned, shift, 1) if shift else turned
                at_row = ((h * size_x + x) * size_y + y) * size_z
                table[at_row : at_row + size_z, :] = jnp.where(valid, moved, FAR)


def bias_fold(d_scores, inner, dims, lanes):
    size_x, size_y, size_z = inner
    _, pad_y, pad_z = dims
    total = None
    for x in range(size_x):
        for y in range(size_y):
            at_row = (x * size_y + y) * size_z
            shift = (x * pad_y + y) * pad_z
            part = d_scores[at_row : at_row + size_z, :]
            part = pltpu.roll(part, lanes - shift, 1) if shift else part
            total = part if total is None else total + part
    rows = size_z
    while rows > 8:
        rows //= 2
        total = total[:rows] + pltpu.roll(total[rows:], lanes - rows, 1)
    step = rows // 2
    while step >= 1:
        moved = pltpu.roll(total, lanes - step, 1)
        total = total + pltpu.roll(moved, rows - step, 0)
        step //= 2
    return total[0:1]


def normed(x, gain):
    inverse = lax.rsqrt(jnp.mean(x * x, axis=-1, keepdims=True) + 1e-06)
    scaled = x * inverse
    return (scaled * gain).astype(BF), scaled, inverse


def attention_grads(
    padded, local, gain, project_ref, output_ref, go, table, probs_s, low_s, inner, dims, heads, send_hidden
):
    lanes, channels = padded.shape
    rows = local.shape[0]
    head = channels // heads
    scale = head ** (-0.5)
    hidden, scaled, _ = normed(padded, gain)
    hidden_l, scaled_l, inverse_l = normed(local, gain)
    keys = jnp.dot(hidden, project_ref[:, channels : 2 * channels], preferred_element_type=F32).astype(BF)
    values = jnp.dot(hidden, project_ref[:, 2 * channels :], preferred_element_type=F32).astype(BF)
    queries = jnp.dot(hidden_l, project_ref[:, :channels], preferred_element_type=F32).astype(BF)
    d_att = dot(go, output_ref[...], (1, 1)).astype(BF)
    column = lax.broadcasted_iota(jnp.int32, (1, channels), 1)
    attended = jnp.zeros((rows, channels), F32)
    d_query = jnp.zeros((rows, channels), F32)
    query_parts, grad_parts, bias_parts = [], [], []
    for h in range(heads):
        mine = (column >= h * head) & (column < (h + 1) * head)
        q = jnp.where(mine, queries.astype(F32), 0.0).astype(BF)
        da = jnp.where(mine, d_att.astype(F32), 0.0).astype(BF)
        query_parts.append(q)
        grad_parts.append(da)
        span = slice(h * rows, (h + 1) * rows)
        scores = dot(q, keys, (1, 1)) * scale + table[span, :]
        weights = jnp.exp(scores - jnp.max(scores, axis=1, keepdims=True))
        probs = weights * (1.0 / jnp.sum(weights, axis=1, keepdims=True))
        probs_low = probs.astype(BF)
        probs_s[span, :] = probs_low
        gathered = jnp.dot(probs_low, values, preferred_element_type=F32)
        gathered = jnp.where(mine, gathered, 0.0).astype(BF).astype(F32)
        attended = attended + gathered
        centre = jnp.sum(da.astype(F32) * gathered, axis=1, keepdims=True)
        d_scores = probs * (dot(da, values, (1, 1)) - centre)
        bias_parts.append(bias_fold(d_scores, inner, dims, lanes))
        low = (d_scores * scale).astype(BF)
        low_s[span, :] = low
        d_query = d_query + jnp.where(mine, jnp.dot(low, keys, preferred_element_type=F32), 0.0)
    attended = attended.astype(BF)
    d_keys = dot(low_s[...], jnp.concatenate(query_parts, axis=0), (0, 0)).astype(BF)
    d_values = dot(probs_s[...], jnp.concatenate(grad_parts, axis=0), (0, 0)).astype(BF)
    d_query = d_query.astype(BF)
    d_hidden = dot(d_keys, project_ref[:, channels : 2 * channels], (1, 1)) + dot(
        d_values, project_ref[:, 2 * channels :], (1, 1)
    )
    send_hidden(d_hidden)
    d_hidden_l = dot(d_query, project_ref[:, :channels], (1, 1))
    project = (
        dot(hidden_l, d_query, (0, 0)),
        dot(hidden, d_keys, (0, 0)),
        dot(hidden, d_values, (0, 0)),
    )
    output = dot(attended, go, (0, 0))
    gain_sum = jnp.sum(d_hidden * scaled, axis=0, keepdims=True) + jnp.sum(
        d_hidden_l * scaled_l, axis=0, keepdims=True
    )
    folded = jnp.concatenate(bias_parts + [jnp.zeros((8 - heads, lanes), F32)], axis=0)
    bias_sum = lax.dot_general(
        folded,
        one_hot(dims, lanes),
        (((1,), (1,)), ((), ())),
        precision=lax.Precision.HIGHEST,
        preferred_element_type=F32,
    )
    return d_hidden, d_hidden_l, project, output, gain_sum, bias_sum, scaled_l, inverse_l


MESH = pl.DeviceIdType.MESH
AXES = ("gx", "gy", "gz")
TURNS = [(x, y, z) for x in (0, -1, 1) for y in (0, -1, 1) for z in (0, -1, 1)][1:]
FLAT = [turn for turn in TURNS if turn[2] == 0]
EDGES = [turn for turn in TURNS if turn[2] != 0]


def span_of(turn, size):
    return {0: (0, size), 1: (size - RADIUS, size), -1: (0, RADIUS)}[turn]


def rim_of(turn, size):
    return {
        0: (RADIUS, size + RADIUS),
        1: (size + RADIUS, size + 2 * RADIUS),
        -1: (0, RADIUS),
    }[turn]


def kernel(
    inner, dims, sizes, factor, chunk,
    tokens_hbm, gain_hbm, project_hbm, output_hbm, bias_hbm, go_hbm,
    token_out, project_out, output_out, gain_out, bias_out,
    table, probs_s, low_s, spread,
    edge_f, edge, main, rims, padded, hidden_f, pack_f, out_main, out_edge, in_main, in_edge,
    sums_f, sums, parts, final,
    tokens_ref, gain_ref, project_ref, output_ref, bias_ref, go_ref,
    tok_send, tok_recv, ret_send, ret_recv, rs_send, rs_recv, ag_send, ag_recv, in_sem,
):
    fetches = [
        pltpu.make_async_copy(source, target, in_sem.at[n])
        for n, (source, target) in enumerate((
            (tokens_hbm, tokens_ref), (bias_hbm, bias_ref), (gain_hbm, gain_ref),
            (project_hbm, project_ref), (output_hbm, output_ref), (go_hbm, go_ref),
        ))
    ]
    for fetch in fetches:
        fetch.start()
    size_x, size_y, size_z = inner
    pad_x, pad_y, pad_z = dims
    rows = size_x * size_y * size_z
    lanes, channels = padded.shape
    heads = bias_ref.shape[0]
    here = [lax.axis_index(axis) for axis in AXES]
    count = sizes[0] * sizes[1] * sizes[2]
    me = (here[0] * sizes[1] + here[1]) * sizes[2] + here[2]

    def peer(k):
        other = lax.rem(me + k, count)
        rest = lax.div(other, sizes[2])
        place = (lax.div(rest, sizes[1]), lax.rem(rest, sizes[1]), lax.rem(other, sizes[2]))
        return other, dict(zip(AXES, place))

    def exists(turn, sign):
        ok = None
        for at, size, step in zip(here, sizes, turn):
            if step:
                this = (at + sign * step >= 0) & (at + sign * step < size)
                ok = this if ok is None else ok & this
        return ok

    def neighbour(turn):
        return {axis: at + step for axis, at, step in zip(AXES, here, turn)}

    main[...] = jnp.zeros_like(main)
    rims[...] = jnp.zeros_like(rims)
    in_main[...] = jnp.zeros_like(in_main)
    in_edge[...] = jnp.zeros_like(in_edge)
    barrier = pltpu.get_barrier_semaphore()

    def greet(k, carry):
        pl.semaphore_signal(barrier, inc=1, device_id=peer(k)[1], device_id_type=MESH)
        return carry

    lax.fori_loop(1, count, greet, 0)
    fetches[0].wait()
    for x in range(size_x):
        for y in range(size_y):
            line = tokens_ref[x, y].astype(F32)
            at = (x * size_y + y) * RADIUS
            edge_f[0, at : at + RADIUS, :] = line[:RADIUS]
            edge_f[1, at : at + RADIUS, :] = line[size_z - RADIUS :]
    edge[...] = edge_f[...].astype(BF)
    pl.semaphore_wait(barrier, count - 1)

    def token_copy(turn):
        n = TURNS.index(turn)
        if turn[2]:
            source = edge.at[1 if turn[2] > 0 else 0]
            target = rims.at[EDGES.index(turn)]
        else:
            (x0, x1), (y0, y1) = (span_of(t, s) for t, s in zip(turn[:2], inner[:2]))
            (u0, u1), (v0, v1) = (rim_of(-t, s) for t, s in zip(turn[:2], inner[:2]))
            source = tokens_ref.at[x0:x1, y0:y1]
            target = main.at[u0:u1, v0:v1]
        return pltpu.make_async_remote_copy(
            src_ref=source, dst_ref=target, send_sem=tok_send.at[n], recv_sem=tok_recv.at[n],
            device_id=neighbour(turn), device_id_type=MESH,
        )

    def grad_copy(turn):
        n = TURNS.index(turn)
        if turn[2]:
            source, target = (buffer.at[EDGES.index(turn)] for buffer in (out_edge, in_edge))
        else:
            (u0, u1), (v0, v1) = (rim_of(t, s) for t, s in zip(turn[:2], inner[:2]))
            source = out_main.at[u0:u1, v0:v1]
            target = in_main.at[FLAT.index(turn), 0 : u1 - u0, 0 : v1 - v0]
        return pltpu.make_async_remote_copy(
            src_ref=source, dst_ref=target, send_sem=ret_send.at[n], recv_sem=ret_recv.at[n],
            device_id=neighbour(turn), device_id_type=MESH,
        )

    def every(make, sign, what):
        for turn in TURNS:
            pl.when(exists(turn, sign))(lambda turn=turn: getattr(make(turn), what)())

    every(token_copy, 1, "start")
    fetches[1].wait()
    bias_table(
        bias_ref, spread, table, inner, dims, lanes,
        [(at, size * cells) for at, size, cells in zip(here, sizes, inner)],
    )
    for fetch in fetches[2:]:
        fetch.wait()
    every(token_copy, -1, "wait_recv")

    filled = pad_x * pad_y * pad_z
    if filled < lanes:
        padded[filled:, :] = jnp.zeros((lanes - filled, channels), F32)
    sides = [
        [(t, u - rim_of(-t, s)[0] + span_of(t, s)[0]) for u in range(s + 2 * RADIUS)
         for t in (0, 1, -1) if rim_of(-t, s)[0] <= u < rim_of(-t, s)[1]]
        for s in inner[:2]
    ]
    for u in range(pad_x):
        for v in range(pad_y):
            (turn_x, x), (turn_y, y) = sides[0][u], sides[1][v]
            at = (u * pad_y + v) * pad_z
            own = turn_x == 0 and turn_y == 0
            line = tokens_ref[x, y] if own else main[u, v]
            padded[at + RADIUS : at + RADIUS + size_z, :] = line.astype(F32)
            row = (x * size_y + y) * RADIUS
            for turn_z, to in ((1, at), (-1, at + RADIUS + size_z)):
                tile = rims[EDGES.index((turn_x, turn_y, turn_z))].astype(F32)
                padded[to : to + RADIUS, :] = tile[row : row + RADIUS]

    def send_hidden(d_hidden):
        hidden_f[...] = d_hidden
        pack_f[...] = jnp.zeros_like(pack_f)
        for u in range(pad_x):
            for v in range(pad_y):
                (turn_x, x), (turn_y, y) = sides[0][u], sides[1][v]
                at = (u * pad_y + v) * pad_z
                out_main[u, v] = hidden_f[at + RADIUS : at + RADIUS + size_z, :].astype(BF)
                row = (x * size_y + y) * RADIUS
                for turn_z, to in ((-1, at), (1, at + RADIUS + size_z)):
                    slot = EDGES.index((-turn_x, -turn_y, turn_z))
                    pack_f[slot, row : row + RADIUS, :] = hidden_f[to : to + RADIUS, :]
        out_edge[...] = pack_f[...].astype(BF)
        every(grad_copy, 1, "start")

    _, d_hidden_l, project, output, gain_sum, bias_sum, scaled, inverse = attention_grads(
        padded[...], tokens_ref[...].astype(F32).reshape(rows, channels), gain_ref[...],
        project_ref, output_ref, go_ref[...], table, probs_s, low_s, inner, dims, heads,
        send_hidden,
    )
    used = 4 * channels
    blocks = project + (output,)
    full = jnp.concatenate(blocks, axis=0).astype(BF)
    if count * chunk > used:
        full = jnp.concatenate([full, jnp.zeros((count * chunk - used, channels), BF)], axis=0)
    sums[:, 0:chunk, :] = full.reshape(count, chunk, channels)
    sums_f[0:8, :] = bias_sum
    sums_f[8:16, :] = jnp.broadcast_to(gain_sum, (8, channels))
    sums[:, chunk:, :] = jnp.broadcast_to(sums_f[...].astype(BF)[None], (count, 16, channels))

    def part_copy(k):
        other, place = peer(k)
        return pltpu.make_async_remote_copy(
            src_ref=sums.at[other], dst_ref=parts.at[me], send_sem=rs_send.at[k],
            recv_sem=rs_recv.at[k], device_id=place, device_id_type=MESH,
        )

    def part_arrival(k):
        other = lax.rem(me + count - k, count)
        return pltpu.make_async_remote_copy(
            src_ref=sums.at[other], dst_ref=parts.at[other], send_sem=rs_send.at[k],
            recv_sem=rs_recv.at[k], device_id=peer(k)[1], device_id_type=MESH,
        )

    def whole_copy(k):
        place = peer(k)[1]
        return pltpu.make_async_remote_copy(
            src_ref=final.at[me], dst_ref=final.at[me], send_sem=ag_send.at[k],
            recv_sem=ag_recv.at[k], device_id=place, device_id_type=MESH,
        )

    def whole_arrival(k):
        other = lax.rem(me + count - k, count)
        return pltpu.make_async_remote_copy(
            src_ref=final.at[other], dst_ref=final.at[other], send_sem=ag_send.at[k],
            recv_sem=ag_recv.at[k], device_id=peer(k)[1], device_id_type=MESH,
        )

    def loop(body):
        lax.fori_loop(1, count, lambda k, carry: (body(k), carry)[1], 0)

    loop(lambda k: part_copy(k).start())
    parts[me] = sums[me]

    every(grad_copy, -1, "wait_recv")
    norm_scaled = d_hidden_l
    low = jnp.zeros(in_edge.shape[1:], F32)
    high = jnp.zeros(in_edge.shape[1:], F32)
    for n, turn in enumerate(EDGES):
        if turn[2] > 0:
            low = low + in_edge[n].astype(F32)
        else:
            high = high + in_edge[n].astype(F32)
    for x in range(size_x):
        for y in range(size_y):
            at = ((x + RADIUS) * pad_y + y + RADIUS) * pad_z + RADIUS
            line = hidden_f[at : at + size_z, :]
            for n, (turn_x, turn_y, _) in enumerate(FLAT):
                (x0, x1), (y0, y1) = span_of(-turn_x, size_x), span_of(-turn_y, size_y)
                if x0 <= x < x1 and y0 <= y < y1:
                    line = line + in_main[n, x - x0, y - y0].astype(F32)
            to = (x * size_y + y) * size_z
            row = (x * size_y + y) * RADIUS
            padded[to : to + size_z, :] = line
            padded[to : to + RADIUS, :] += low[row : row + RADIUS]
            padded[to + size_z - RADIUS : to + size_z, :] += high[row : row + RADIUS]
    d_scaled = (padded[0:rows, :] + norm_scaled) * gain_ref[...]
    token_grad = inverse * (
        d_scaled - scaled * jnp.mean(d_scaled * scaled, axis=-1, keepdims=True)
    )
    token_out[...] = token_grad.reshape(inner + (channels,))

    loop(lambda k: part_arrival(k).wait_recv())
    total = lax.fori_loop(
        1, count, lambda k, carry: carry + parts[k].astype(F32), parts[0].astype(F32)
    ) * factor
    final[me] = total[0:chunk].astype(BF)
    loop(lambda k: whole_copy(k).start())
    loop(lambda k: whole_arrival(k).wait_recv())
    done = final[...].astype(F32).reshape(count * chunk, channels)
    for i in range(3):
        project_out[:, i * channels : (i + 1) * channels] = done[i * channels : (i + 1) * channels]
    output_out[...] = done[3 * channels : used]
    bias_out[...] = total[chunk : chunk + heads, : WIN**3]
    gain_out[...] = total[chunk + 8 : chunk + 9]
    every(token_copy, 1, "wait_send")
    every(grad_copy, 1, "wait_send")
    loop(lambda k: part_copy(k).wait_send())
    loop(lambda k: whole_copy(k).wait_send())


def write_out(*refs):
    sources, targets, sem = list(refs[:5]), refs[5:10], refs[10]
    sources[3] = sources[3].at[0]
    copies = [
        pltpu.make_async_copy(source, target, sem.at[n])
        for n, (source, target) in enumerate(zip(sources, targets))
    ]
    for copy in copies:
        copy.start()
    for copy in copies:
        copy.wait()


def shards(tokens, norm_gain, project_weight, output_weight, position_bias, grad_output):
    inner, channels = tokens.shape[:3], tokens.shape[3]
    heads = position_bias.shape[0]
    sizes = tuple(lax.axis_size(axis) for axis in AXES)
    dims = tuple(size + 2 * RADIUS for size in inner)
    rows = inner[0] * inner[1] * inner[2]
    lanes = -(-dims[0] * dims[1] * dims[2] // 128) * 128
    count = sizes[0] * sizes[1] * sizes[2]
    factor = (rows * count) ** (-0.5)
    chunk = -(-4 * channels // (16 * count)) * 16
    tile = inner[0] * inner[1] * RADIUS
    vmem = pl.BlockSpec(memory_space=pltpu.VMEM)
    many = len(TURNS)
    out = pl.pallas_call(
        functools.partial(kernel, inner, dims, sizes, factor, chunk),
        out_shape=(
            jax.ShapeDtypeStruct(tokens.shape, F32),
            jax.ShapeDtypeStruct((channels, 3 * channels), F32),
            jax.ShapeDtypeStruct((channels, channels), F32),
            jax.ShapeDtypeStruct((1, channels), F32),
            jax.ShapeDtypeStruct(position_bias.shape, F32),
        ),
        in_specs=[pl.BlockSpec(memory_space=pltpu.HBM)] * 6,
        out_specs=(vmem,) * 5,
        scratch_shapes=[
            pltpu.VMEM((heads * rows, lanes), F32),
            pltpu.VMEM((heads * rows, lanes), BF),
            pltpu.VMEM((heads * rows, lanes), BF),
            pltpu.VMEM((8, 128), F32),
            pltpu.VMEM((2, tile, channels), F32),
            pltpu.VMEM((2, tile, channels), BF),
            pltpu.VMEM((dims[0], dims[1], inner[2], channels), BF),
            pltpu.VMEM((len(EDGES), tile, channels), BF),
            pltpu.VMEM((lanes, channels), F32),
            pltpu.VMEM((lanes, channels), F32),
            pltpu.VMEM((len(EDGES), tile, channels), F32),
            pltpu.VMEM((dims[0], dims[1], inner[2], channels), BF),
            pltpu.VMEM((len(EDGES), tile, channels), BF),
            pltpu.VMEM((len(FLAT),) + inner + (channels,), BF),
            pltpu.VMEM((len(EDGES), tile, channels), BF),
            pltpu.VMEM((16, channels), F32),
            pltpu.VMEM((count, chunk + 16, channels), BF),
            pltpu.VMEM((count, chunk + 16, channels), BF),
            pltpu.VMEM((count, chunk, channels), BF),
            pltpu.VMEM(tokens.shape, BF),
            pltpu.VMEM((1, channels), F32),
            pltpu.VMEM(project_weight.shape, BF),
            pltpu.VMEM(output_weight.shape, BF),
            pltpu.VMEM(position_bias.shape, F32),
            pltpu.VMEM((rows, channels), BF),
        ]
        + [pltpu.SemaphoreType.DMA((many,))] * 4
        + [pltpu.SemaphoreType.DMA((count,))] * 4
        + [pltpu.SemaphoreType.DMA((6,))],
        compiler_params=pltpu.CompilerParams(
            vmem_limit_bytes=62 * 2**20, collective_id=0, has_side_effects=True
        ),
    )(
        tokens,
        norm_gain.reshape(1, channels),
        project_weight,
        output_weight,
        position_bias,
        grad_output.reshape(rows, channels),
    )
    results = pl.pallas_call(
        write_out,
        out_shape=tuple(
            jax.ShapeDtypeStruct((channels,) if n == 3 else part.shape, F32)
            for n, part in enumerate(out)
        ),
        in_specs=[pl.BlockSpec(memory_space=pltpu.HBM)] * 5,
        out_specs=(pl.BlockSpec(memory_space=pltpu.HBM),) * 5,
        scratch_shapes=[pltpu.SemaphoreType.DMA((5,))],
        compiler_params=pltpu.CompilerParams(vmem_limit_bytes=62 * 2**20),
    )(*out)
    return tuple(results)


def solution(mesh):
    tokens = P(("groups", "gx"), "gy", "gz", None)
    return jax.shard_map(
        shards,
        mesh=mesh,
        in_specs=(tokens, P(), P(), P(), P(), tokens),
        out_specs=(tokens, P("groups", None), P("groups", None), P("groups"), P("groups", None)),
        check_vma=False,
    )
```

```python
import functools

import jax
import jax.numpy as jnp
from jax import lax
from jax.experimental import pallas as pl
from jax.experimental.pallas import tpu as pltpu
from jax.sharding import PartitionSpec as P

WIN = 5
RADIUS = 2
FAR = -1e30
BF = jnp.bfloat16
F32 = jnp.float32


def dot(a, b, over):
    return lax.dot_general(a, b, ((over[:1], over[1:]), ((), ())), preferred_element_type=F32)


def digits(index, steps):
    out = []
    for step, count in steps:
        digit = jnp.zeros_like(index)
        for i in range(1, count):
            digit = digit + (index >= step * i).astype(jnp.int32)
        index = index - digit * step
        out.append(digit)
    return out


def one_hot(dims, lanes):
    _, pad_y, pad_z = dims
    rows = lax.broadcasted_iota(jnp.int32, (128, 1), 0)
    i, j, l = digits(rows, ((WIN * WIN, WIN + 1), (WIN, WIN), (1, WIN)))
    code = jnp.where(rows < WIN**3, (i * pad_y + j) * pad_z + l, -1)
    return (lax.broadcasted_iota(jnp.int32, (128, lanes), 1) == code).astype(F32)


def bias_table(bias_ref, spread, table, inner, dims, lanes, extents):
    heads = bias_ref.shape[0]
    size_x, size_y, size_z = inner
    pad_x, pad_y, pad_z = dims
    spread[...] = jnp.zeros_like(spread)
    spread[0:heads, 0 : WIN**3] = bias_ref[...]
    base = lax.dot_general(
        spread[...],
        one_hot(dims, lanes),
        (((1,), (0,)), ((), ())),
        precision=lax.Precision.HIGHEST,
        preferred_element_type=F32,
    )
    lane = lax.broadcasted_iota(jnp.int32, (1, lanes), 1)
    at = digits(lane, ((pad_y * pad_z, pad_x + 2), (pad_z, pad_y), (1, pad_z)))
    near = (at[0] < WIN) & (at[1] < WIN) & (at[2] < WIN)
    base = jnp.where(near, base, FAR)
    valid = lane < pad_x * pad_y * pad_z
    for digit, size, (place, extent) in zip(at, inner, extents):
        position = digit + (place * size - RADIUS)
        valid = valid & (position >= 0) & (position < extent)
    row = lax.broadcasted_iota(jnp.int32, (size_z, 1), 0)
    for h in range(heads):
        turned = jnp.broadcast_to(base[h : h + 1], (size_z, lanes))
        bit = 1
        while bit < size_z:
            turned = jnp.where((row & bit) > 0, pltpu.roll(turned, bit, 1), turned)
            bit *= 2
        for x in range(size_x):
            for y in range(size_y):
                shift = (x * pad_y + y) * pad_z
                moved = pltpu.roll(turned, shift, 1) if shift else turned
                at_row = ((h * size_x + x) * size_y + y) * size_z
                table[at_row : at_row + size_z, :] = jnp.where(valid, moved, FAR)


def bias_fold(d_scores, inner, dims, lanes):
    size_x, size_y, size_z = inner
    _, pad_y, pad_z = dims
    total = None
    for x in range(size_x):
        for y in range(size_y):
            at_row = (x * size_y + y) * size_z
            shift = (x * pad_y + y) * pad_z
            part = d_scores[at_row : at_row + size_z, :]
            part = pltpu.roll(part, lanes - shift, 1) if shift else part
            total = part if total is None else total + part
    rows = size_z
    while rows > 8:
        rows //= 2
        total = total[:rows] + pltpu.roll(total[rows:], lanes - rows, 1)
    step = rows // 2
    while step >= 1:
        moved = pltpu.roll(total, lanes - step, 1)
        total = total + pltpu.roll(moved, rows - step, 0)
        step //= 2
    return total[0:1]


def normed(x, gain):
    inverse = lax.rsqrt(jnp.mean(x * x, axis=-1, keepdims=True) + 1e-06)
    scaled = x * inverse
    return (scaled * gain).astype(BF), scaled, inverse


def attention_grads(
    padded, local, gain, project_ref, output_ref, go, table, probs_s, low_s, inner, dims, heads, send_hidden
):
    lanes, channels = padded.shape
    rows = local.shape[0]
    head = channels // heads
    scale = head ** (-0.5)
    hidden, scaled, _ = normed(padded, gain)
    hidden_l, scaled_l, inverse_l = normed(local, gain)
    keys = jnp.dot(hidden, project_ref[:, channels : 2 * channels], preferred_element_type=F32).astype(BF)
    values = jnp.dot(hidden, project_ref[:, 2 * channels :], preferred_element_type=F32).astype(BF)
    queries = jnp.dot(hidden_l, project_ref[:, :channels], preferred_element_type=F32).astype(BF)
    d_att = dot(go, output_ref[...], (1, 1)).astype(BF)
    column = lax.broadcasted_iota(jnp.int32, (1, channels), 1)
    attended = jnp.zeros((rows, channels), F32)
    d_query = jnp.zeros((rows, channels), F32)
    query_parts, grad_parts, bias_parts = [], [], []
    for h in range(heads):
        mine = (column >= h * head) & (column < (h + 1) * head)
        q = jnp.where(mine, queries.astype(F32), 0.0).astype(BF)
        da = jnp.where(mine, d_att.astype(F32), 0.0).astype(BF)
        query_parts.append(q)
        grad_parts.append(da)
        span = slice(h * rows, (h + 1) * rows)
        scores = dot(q, keys, (1, 1)) * scale + table[span, :]
        weights = jnp.exp(scores - jnp.max(scores, axis=1, keepdims=True))
        probs = weights * (1.0 / jnp.sum(weights, axis=1, keepdims=True))
        probs_low = probs.astype(BF)
        probs_s[span, :] = probs_low
        gathered = jnp.dot(probs_low, values, preferred_element_type=F32)
        gathered = jnp.where(mine, gathered, 0.0).astype(BF).astype(F32)
        attended = attended + gathered
        centre = jnp.sum(da.astype(F32) * gathered, axis=1, keepdims=True)
        d_scores = probs * (dot(da, values, (1, 1)) - centre)
        bias_parts.append(bias_fold(d_scores, inner, dims, lanes))
        low = (d_scores * scale).astype(BF)
        low_s[span, :] = low
        d_query = d_query + jnp.where(mine, jnp.dot(low, keys, preferred_element_type=F32), 0.0)
    attended = attended.astype(BF)
    d_keys = dot(low_s[...], jnp.concatenate(query_parts, axis=0), (0, 0)).astype(BF)
    d_values = dot(probs_s[...], jnp.concatenate(grad_parts, axis=0), (0, 0)).astype(BF)
    d_query = d_query.astype(BF)
    d_hidden = dot(d_keys, project_ref[:, channels : 2 * channels], (1, 1)) + dot(
        d_values, project_ref[:, 2 * channels :], (1, 1)
    )
    send_hidden(d_hidden)
    d_hidden_l = dot(d_query, project_ref[:, :channels], (1, 1))
    project = (
        dot(hidden_l, d_query, (0, 0)),
        dot(hidden, d_keys, (0, 0)),
        dot(hidden, d_values, (0, 0)),
    )
    output = dot(attended, go, (0, 0))
    gain_sum = jnp.sum(d_hidden * scaled, axis=0, keepdims=True) + jnp.sum(
        d_hidden_l * scaled_l, axis=0, keepdims=True
    )
    folded = jnp.concatenate(bias_parts + [jnp.zeros((8 - heads, lanes), F32)], axis=0)
    bias_sum = lax.dot_general(
        folded,
        one_hot(dims, lanes),
        (((1,), (1,)), ((), ())),
        precision=lax.Precision.HIGHEST,
        preferred_element_type=F32,
    )
    return d_hidden, d_hidden_l, project, output, gain_sum, bias_sum, scaled_l, inverse_l


MESH = pl.DeviceIdType.MESH
AXES = ("gx", "gy", "gz")
TURNS = [(x, y, z) for x in (0, -1, 1) for y in (0, -1, 1) for z in (0, -1, 1)][1:]
FLAT = [turn for turn in TURNS if turn[2] == 0]
EDGES = [turn for turn in TURNS if turn[2] != 0]


def span_of(turn, size):
    return {0: (0, size), 1: (size - RADIUS, size), -1: (0, RADIUS)}[turn]


def rim_of(turn, size):
    return {
        0: (RADIUS, size + RADIUS),
        1: (size + RADIUS, size + 2 * RADIUS),
        -1: (0, RADIUS),
    }[turn]


def kernel(
    inner, dims, sizes, factor, chunk,
    tokens_hbm, gain_hbm, project_hbm, output_hbm, bias_hbm, go_hbm,
    token_out, project_out, output_out, gain_out, bias_out,
    table, probs_s, low_s, spread,
    edge_f, edge, main, rims, padded, hidden_f, pack_f, out_main, out_edge, in_main, in_edge,
    sums_f, sums, parts, final,
    tokens_ref, gain_ref, project_ref, output_ref, bias_ref, go_ref,
    tok_send, tok_recv, ret_send, ret_recv, rs_send, rs_recv, ag_send, ag_recv, in_sem,
):
    fetches = [
        pltpu.make_async_copy(source, target, in_sem.at[n])
        for n, (source, target) in enumerate((
            (tokens_hbm, tokens_ref), (bias_hbm, bias_ref), (gain_hbm, gain_ref),
            (project_hbm, project_ref), (output_hbm, output_ref), (go_hbm, go_ref),
        ))
    ]
    for fetch in fetches:
        fetch.start()
    size_x, size_y, size_z = inner
    pad_x, pad_y, pad_z = dims
    rows = size_x * size_y * size_z
    lanes, channels = padded.shape
    heads = bias_ref.shape[0]
    here = [lax.axis_index(axis) for axis in AXES]
    count = sizes[0] * sizes[1] * sizes[2]
    me = (here[0] * sizes[1] + here[1]) * sizes[2] + here[2]

    def peer(k):
        other = lax.rem(me + k, count)
        rest = lax.div(other, sizes[2])
        place = (lax.div(rest, sizes[1]), lax.rem(rest, sizes[1]), lax.rem(other, sizes[2]))
        return other, dict(zip(AXES, place))

    def exists(turn, sign):
        ok = None
        for at, size, step in zip(here, sizes, turn):
            if step:
                this = (at + sign * step >= 0) & (at + sign * step < size)
                ok = this if ok is None else ok & this
        return ok

    def neighbour(turn):
        return {axis: at + step for axis, at, step in zip(AXES, here, turn)}

    main[...] = jnp.zeros_like(main)
    rims[...] = jnp.zeros_like(rims)
    in_main[...] = jnp.zeros_like(in_main)
    in_edge[...] = jnp.zeros_like(in_edge)
    barrier = pltpu.get_barrier_semaphore()

    def greet(k, carry):
        pl.semaphore_signal(barrier, inc=1, device_id=peer(k)[1], device_id_type=MESH)
        return carry

    lax.fori_loop(1, count, greet, 0)
    fetches[0].wait()
    for x in range(size_x):
        for y in range(size_y):
            line = tokens_ref[x, y].astype(F32)
            at = (x * size_y + y) * RADIUS
            edge_f[0, at : at + RADIUS, :] = line[:RADIUS]
            edge_f[1, at : at + RADIUS, :] = line[size_z - RADIUS :]
    edge[...] = edge_f[...].astype(BF)
    pl.semaphore_wait(barrier, count - 1)

    def token_copy(turn):
        n = TURNS.index(turn)
        if turn[2]:
            source = edge.at[1 if turn[2] > 0 else 0]
            target = rims.at[EDGES.index(turn)]
        else:
            (x0, x1), (y0, y1) = (span_of(t, s) for t, s in zip(turn[:2], inner[:2]))
            (u0, u1), (v0, v1) = (rim_of(-t, s) for t, s in zip(turn[:2], inner[:2]))
            source = tokens_ref.at[x0:x1, y0:y1]
            target = main.at[u0:u1, v0:v1]
        return pltpu.make_async_remote_copy(
            src_ref=source, dst_ref=target, send_sem=tok_send.at[n], recv_sem=tok_recv.at[n],
            device_id=neighbour(turn), device_id_type=MESH,
        )

    def grad_copy(turn):
        n = TURNS.index(turn)
        if turn[2]:
            source, target = (buffer.at[EDGES.index(turn)] for buffer in (out_edge, in_edge))
        else:
            (u0, u1), (v0, v1) = (rim_of(t, s) for t, s in zip(turn[:2], inner[:2]))
            source = out_main.at[u0:u1, v0:v1]
            target = in_main.at[FLAT.index(turn), 0 : u1 - u0, 0 : v1 - v0]
        return pltpu.make_async_remote_copy(
            src_ref=source, dst_ref=target, send_sem=ret_send.at[n], recv_sem=ret_recv.at[n],
            device_id=neighbour(turn), device_id_type=MESH,
        )

    def every(make, sign, what):
        for turn in TURNS:
            pl.when(exists(turn, sign))(lambda turn=turn: getattr(make(turn), what)())

    every(token_copy, 1, "start")
    fetches[1].wait()
    bias_table(
        bias_ref, spread, table, inner, dims, lanes,
        [(at, size * cells) for at, size, cells in zip(here, sizes, inner)],
    )
    for fetch in fetches[2:]:
        fetch.wait()
    every(token_copy, -1, "wait_recv")

    filled = pad_x * pad_y * pad_z
    if filled < lanes:
        padded[filled:, :] = jnp.zeros((lanes - filled, channels), F32)
    sides = [
        [(t, u - rim_of(-t, s)[0] + span_of(t, s)[0]) for u in range(s + 2 * RADIUS)
         for t in (0, 1, -1) if rim_of(-t, s)[0] <= u < rim_of(-t, s)[1]]
        for s in inner[:2]
    ]
    for u in range(pad_x):
        for v in range(pad_y):
            (turn_x, x), (turn_y, y) = sides[0][u], sides[1][v]
            at = (u * pad_y + v) * pad_z
            own = turn_x == 0 and turn_y == 0
            line = tokens_ref[x, y] if own else main[u, v]
            padded[at + RADIUS : at + RADIUS + size_z, :] = line.astype(F32)
            row = (x * size_y + y) * RADIUS
            for turn_z, to in ((1, at), (-1, at + RADIUS + size_z)):
                tile = rims[EDGES.index((turn_x, turn_y, turn_z))].astype(F32)
                padded[to : to + RADIUS, :] = tile[row : row + RADIUS]

    def send_hidden(d_hidden):
        hidden_f[...] = d_hidden
        pack_f[...] = jnp.zeros_like(pack_f)
        for u in range(pad_x):
            for v in range(pad_y):
                (turn_x, x), (turn_y, y) = sides[0][u], sides[1][v]
                at = (u * pad_y + v) * pad_z
                out_main[u, v] = hidden_f[at + RADIUS : at + RADIUS + size_z, :].astype(BF)
                row = (x * size_y + y) * RADIUS
                for turn_z, to in ((-1, at), (1, at + RADIUS + size_z)):
                    slot = EDGES.index((-turn_x, -turn_y, turn_z))
                    pack_f[slot, row : row + RADIUS, :] = hidden_f[to : to + RADIUS, :]
        out_edge[...] = pack_f[...].astype(BF)
        every(grad_copy, 1, "start")

    _, d_hidden_l, project, output, gain_sum, bias_sum, scaled, inverse = attention_grads(
        padded[...], tokens_ref[...].astype(F32).reshape(rows, channels), gain_ref[...],
        project_ref, output_ref, go_ref[...], table, probs_s, low_s, inner, dims, heads,
        send_hidden,
    )
    used = 4 * channels
    blocks = project + (output,)
    full = jnp.concatenate(blocks, axis=0).astype(BF)
    if count * chunk > used:
        full = jnp.concatenate([full, jnp.zeros((count * chunk - used, channels), BF)], axis=0)
    sums[:, 0:chunk, :] = full.reshape(count, chunk, channels)
    sums_f[0:8, :] = bias_sum
    sums_f[8:16, :] = jnp.broadcast_to(gain_sum, (8, channels))
    sums[:, chunk:, :] = jnp.broadcast_to(sums_f[...].astype(BF)[None], (count, 16, channels))

    def part_copy(k):
        other, place = peer(k)
        return pltpu.make_async_remote_copy(
            src_ref=sums.at[other], dst_ref=parts.at[me], send_sem=rs_send.at[k],
            recv_sem=rs_recv.at[k], device_id=place, device_id_type=MESH,
        )

    def part_arrival(k):
        other = lax.rem(me + count - k, count)
        return pltpu.make_async_remote_copy(
            src_ref=sums.at[other], dst_ref=parts.at[other], send_sem=rs_send.at[k],
            recv_sem=rs_recv.at[k], device_id=peer(k)[1], device_id_type=MESH,
        )

    def whole_copy(k):
        place = peer(k)[1]
        return pltpu.make_async_remote_copy(
            src_ref=final.at[me], dst_ref=final.at[me], send_sem=ag_send.at[k],
            recv_sem=ag_recv.at[k], device_id=place, device_id_type=MESH,
        )

    def whole_arrival(k):
        other = lax.rem(me + count - k, count)
        return pltpu.make_async_remote_copy(
            src_ref=final.at[other], dst_ref=final.at[other], send_sem=ag_send.at[k],
            recv_sem=ag_recv.at[k], device_id=peer(k)[1], device_id_type=MESH,
        )

    def loop(body):
        lax.fori_loop(1, count, lambda k, carry: (body(k), carry)[1], 0)

    loop(lambda k: part_copy(k).start())
    parts[me] = sums[me]

    every(grad_copy, -1, "wait_recv")
    norm_scaled = d_hidden_l
    low = jnp.zeros(in_edge.shape[1:], F32)
    high = jnp.zeros(in_edge.shape[1:], F32)
    for n, turn in enumerate(EDGES):
        if turn[2] > 0:
            low = low + in_edge[n].astype(F32)
        else:
            high = high + in_edge[n].astype(F32)
    for x in range(size_x):
        for y in range(size_y):
            at = ((x + RADIUS) * pad_y + y + RADIUS) * pad_z + RADIUS
            line = hidden_f[at : at + size_z, :]
            for n, (turn_x, turn_y, _) in enumerate(FLAT):
                (x0, x1), (y0, y1) = span_of(-turn_x, size_x), span_of(-turn_y, size_y)
                if x0 <= x < x1 and y0 <= y < y1:
                    line = line + in_main[n, x - x0, y - y0].astype(F32)
            to = (x * size_y + y) * size_z
            row = (x * size_y + y) * RADIUS
            padded[to : to + size_z, :] = line
            padded[to : to + RADIUS, :] += low[row : row + RADIUS]
            padded[to + size_z - RADIUS : to + size_z, :] += high[row : row + RADIUS]
    d_scaled = (padded[0:rows, :] + norm_scaled) * gain_ref[...]
    token_grad = inverse * (
        d_scaled - scaled * jnp.mean(d_scaled * scaled, axis=-1, keepdims=True)
    )
    token_out[...] = token_grad.reshape(inner + (channels,))

    loop(lambda k: part_arrival(k).wait_recv())
    total = lax.fori_loop(
        1, count, lambda k, carry: carry + parts[k].astype(F32), parts[0].astype(F32)
    ) * factor
    final[me] = total[0:chunk].astype(BF)
    loop(lambda k: whole_copy(k).start())
    loop(lambda k: whole_arrival(k).wait_recv())
    done = final[...].astype(F32).reshape(count * chunk, channels)
    for i in range(3):
        project_out[:, i * channels : (i + 1) * channels] = done[i * channels : (i + 1) * channels]
    output_out[...] = done[3 * channels : used]
    bias_out[...] = total[chunk : chunk + heads, : WIN**3]
    gain_out[...] = total[chunk + 8 : chunk + 9]
    every(token_copy, 1, "wait_send")
    every(grad_copy, 1, "wait_send")
    loop(lambda k: part_copy(k).wait_send())
    loop(lambda k: whole_copy(k).wait_send())


def write_out(*refs):
    sources, targets, held, in_sem, out_sem = refs[:5], list(refs[5:10]), refs[10:15], refs[15], refs[16]
    takes = [pltpu.make_async_copy(sources[n], held[n], in_sem.at[n]) for n in range(5)]
    gives = [
        pltpu.make_async_copy(held[n].at[0] if n == 3 else held[n], targets[n], out_sem.at[n])
        for n in range(5)
    ]
    for copy in takes:
        copy.start()
    for take, give in zip(takes, gives):
        take.wait()
        give.start()
    for copy in gives:
        copy.wait()


def shards(tokens, norm_gain, project_weight, output_weight, position_bias, grad_output):
    inner, channels = tokens.shape[:3], tokens.shape[3]
    heads = position_bias.shape[0]
    sizes = tuple(lax.axis_size(axis) for axis in AXES)
    dims = tuple(size + 2 * RADIUS for size in inner)
    rows = inner[0] * inner[1] * inner[2]
    lanes = -(-dims[0] * dims[1] * dims[2] // 128) * 128
    count = sizes[0] * sizes[1] * sizes[2]
    factor = (rows * count) ** (-0.5)
    chunk = -(-4 * channels // (16 * count)) * 16
    tile = inner[0] * inner[1] * RADIUS
    vmem = pl.BlockSpec(memory_space=pltpu.VMEM)
    many = len(TURNS)
    out = pl.pallas_call(
        functools.partial(kernel, inner, dims, sizes, factor, chunk),
        out_shape=(
            jax.ShapeDtypeStruct(tokens.shape, F32),
            jax.ShapeDtypeStruct((channels, 3 * channels), F32),
            jax.ShapeDtypeStruct((channels, channels), F32),
            jax.ShapeDtypeStruct((1, channels), F32),
            jax.ShapeDtypeStruct(position_bias.shape, F32),
        ),
        in_specs=[pl.BlockSpec(memory_space=pltpu.HBM)] * 6,
        out_specs=(vmem,) * 5,
        scratch_shapes=[
            pltpu.VMEM((heads * rows, lanes), F32),
            pltpu.VMEM((heads * rows, lanes), BF),
            pltpu.VMEM((heads * rows, lanes), BF),
            pltpu.VMEM((8, 128), F32),
            pltpu.VMEM((2, tile, channels), F32),
            pltpu.VMEM((2, tile, channels), BF),
            pltpu.VMEM((dims[0], dims[1], inner[2], channels), BF),
            pltpu.VMEM((len(EDGES), tile, channels), BF),
            pltpu.VMEM((lanes, channels), F32),
            pltpu.VMEM((lanes, channels), F32),
            pltpu.VMEM((len(EDGES), tile, channels), F32),
            pltpu.VMEM((dims[0], dims[1], inner[2], channels), BF),
            pltpu.VMEM((len(EDGES), tile, channels), BF),
            pltpu.VMEM((len(FLAT),) + inner + (channels,), BF),
            pltpu.VMEM((len(EDGES), tile, channels), BF),
            pltpu.VMEM((16, channels), F32),
            pltpu.VMEM((count, chunk + 16, channels), BF),
            pltpu.VMEM((count, chunk + 16, channels), BF),
            pltpu.VMEM((count, chunk, channels), BF),
            pltpu.VMEM(tokens.shape, BF),
            pltpu.VMEM((1, channels), F32),
            pltpu.VMEM(project_weight.shape, BF),
            pltpu.VMEM(output_weight.shape, BF),
            pltpu.VMEM(position_bias.shape, F32),
            pltpu.VMEM((rows, channels), BF),
        ]
        + [pltpu.SemaphoreType.DMA((many,))] * 4
        + [pltpu.SemaphoreType.DMA((count,))] * 4
        + [pltpu.SemaphoreType.DMA((6,))],
        compiler_params=pltpu.CompilerParams(
            vmem_limit_bytes=62 * 2**20, collective_id=0, has_side_effects=True
        ),
    )(
        tokens,
        norm_gain.reshape(1, channels),
        project_weight,
        output_weight,
        position_bias,
        grad_output.reshape(rows, channels),
    )
    results = pl.pallas_call(
        write_out,
        out_shape=tuple(
            jax.ShapeDtypeStruct((channels,) if n == 3 else part.shape, F32)
            for n, part in enumerate(out)
        ),
        in_specs=[pl.BlockSpec(memory_space=pltpu.HBM)] * 5,
        out_specs=(pl.BlockSpec(memory_space=pltpu.HBM),) * 5,
        scratch_shapes=[pltpu.VMEM(part.shape, F32) for part in out]
        + [pltpu.SemaphoreType.DMA((5,))] * 2,
        compiler_params=pltpu.CompilerParams(vmem_limit_bytes=62 * 2**20),
    )(*out)
    return tuple(results)


def solution(mesh):
    tokens = P(("groups", "gx"), "gy", "gz", None)
    return jax.shard_map(
        shards,
        mesh=mesh,
        in_specs=(tokens, P(), P(), P(), P(), tokens),
        out_specs=(tokens, P("groups", None), P("groups", None), P("groups"), P("groups", None)),
        check_vma=False,
    )
```

```python
import functools

import jax
import jax.numpy as jnp
from jax import lax
from jax.experimental import pallas as pl
from jax.experimental.pallas import tpu as pltpu
from jax.sharding import PartitionSpec as P

WIN = 5
RADIUS = 2
FAR = -1e30
BF = jnp.bfloat16
F32 = jnp.float32


def dot(a, b, over):
    return lax.dot_general(a, b, ((over[:1], over[1:]), ((), ())), preferred_element_type=F32)


def digits(index, steps):
    out = []
    for step, count in steps:
        digit = jnp.zeros_like(index)
        for i in range(1, count):
            digit = digit + (index >= step * i).astype(jnp.int32)
        index = index - digit * step
        out.append(digit)
    return out


def one_hot(dims, lanes):
    _, pad_y, pad_z = dims
    rows = lax.broadcasted_iota(jnp.int32, (128, 1), 0)
    i, j, l = digits(rows, ((WIN * WIN, WIN + 1), (WIN, WIN), (1, WIN)))
    code = jnp.where(rows < WIN**3, (i * pad_y + j) * pad_z + l, -1)
    return (lax.broadcasted_iota(jnp.int32, (128, lanes), 1) == code).astype(F32)


def bias_table(bias_ref, spread, table, inner, dims, lanes, extents):
    heads = bias_ref.shape[0]
    size_x, size_y, size_z = inner
    pad_x, pad_y, pad_z = dims
    spread[...] = jnp.zeros_like(spread)
    spread[0:heads, 0 : WIN**3] = bias_ref[...]
    base = lax.dot_general(
        spread[...],
        one_hot(dims, lanes),
        (((1,), (0,)), ((), ())),
        precision=lax.Precision.HIGHEST,
        preferred_element_type=F32,
    )
    lane = lax.broadcasted_iota(jnp.int32, (1, lanes), 1)
    at = digits(lane, ((pad_y * pad_z, pad_x + 2), (pad_z, pad_y), (1, pad_z)))
    near = (at[0] < WIN) & (at[1] < WIN) & (at[2] < WIN)
    base = jnp.where(near, base, FAR)
    valid = lane < pad_x * pad_y * pad_z
    for digit, size, (place, extent) in zip(at, inner, extents):
        position = digit + (place * size - RADIUS)
        valid = valid & (position >= 0) & (position < extent)
    row = lax.broadcasted_iota(jnp.int32, (size_z, 1), 0)
    for h in range(heads):
        turned = jnp.broadcast_to(base[h : h + 1], (size_z, lanes))
        bit = 1
        while bit < size_z:
            turned = jnp.where((row & bit) > 0, pltpu.roll(turned, bit, 1), turned)
            bit *= 2
        for x in range(size_x):
            for y in range(size_y):
                shift = (x * pad_y + y) * pad_z
                moved = pltpu.roll(turned, shift, 1) if shift else turned
                at_row = ((h * size_x + x) * size_y + y) * size_z
                table[at_row : at_row + size_z, :] = jnp.where(valid, moved, FAR)


def bias_fold(d_scores, inner, dims, lanes):
    size_x, size_y, size_z = inner
    _, pad_y, pad_z = dims
    total = None
    for x in range(size_x):
        for y in range(size_y):
            at_row = (x * size_y + y) * size_z
            shift = (x * pad_y + y) * pad_z
            part = d_scores[at_row : at_row + size_z, :]
            part = pltpu.roll(part, lanes - shift, 1) if shift else part
            total = part if total is None else total + part
    rows = size_z
    while rows > 8:
        rows //= 2
        total = total[:rows] + pltpu.roll(total[rows:], lanes - rows, 1)
    step = rows // 2
    while step >= 1:
        moved = pltpu.roll(total, lanes - step, 1)
        total = total + pltpu.roll(moved, rows - step, 0)
        step //= 2
    return total[0:1]


def normed(x, gain):
    inverse = lax.rsqrt(jnp.mean(x * x, axis=-1, keepdims=True) + 1e-06)
    scaled = x * inverse
    return (scaled * gain).astype(BF), scaled, inverse


def attention_grads(
    padded, local, gain, project_ref, output_ref, go, table, probs_s, low_s, inner, dims, heads, send_hidden
):
    lanes, channels = padded.shape
    rows = local.shape[0]
    head = channels // heads
    scale = head ** (-0.5)
    hidden, scaled, _ = normed(padded, gain)
    hidden_l, scaled_l, inverse_l = normed(local, gain)
    keys = jnp.dot(hidden, project_ref[:, channels : 2 * channels], preferred_element_type=F32).astype(BF)
    values = jnp.dot(hidden, project_ref[:, 2 * channels :], preferred_element_type=F32).astype(BF)
    queries = jnp.dot(hidden_l, project_ref[:, :channels], preferred_element_type=F32).astype(BF)
    d_att = dot(go, output_ref[...], (1, 1)).astype(BF)
    column = lax.broadcasted_iota(jnp.int32, (1, channels), 1)
    attended = jnp.zeros((rows, channels), F32)
    d_query = jnp.zeros((rows, channels), F32)
    query_parts, grad_parts, bias_parts = [], [], []
    for h in range(heads):
        mine = (column >= h * head) & (column < (h + 1) * head)
        q = jnp.where(mine, queries.astype(F32), 0.0).astype(BF)
        da = jnp.where(mine, d_att.astype(F32), 0.0).astype(BF)
        query_parts.append(q)
        grad_parts.append(da)
        span = slice(h * rows, (h + 1) * rows)
        scores = dot(q, keys, (1, 1)) * scale + table[span, :]
        weights = jnp.exp(scores - jnp.max(scores, axis=1, keepdims=True))
        probs = weights * (1.0 / jnp.sum(weights, axis=1, keepdims=True))
        probs_low = probs.astype(BF)
        probs_s[span, :] = probs_low
        gathered = jnp.dot(probs_low, values, preferred_element_type=F32)
        gathered = jnp.where(mine, gathered, 0.0).astype(BF).astype(F32)
        attended = attended + gathered
        centre = jnp.sum(da.astype(F32) * gathered, axis=1, keepdims=True)
        d_scores = probs * (dot(da, values, (1, 1)) - centre)
        bias_parts.append(bias_fold(d_scores, inner, dims, lanes))
        low = (d_scores * scale).astype(BF)
        low_s[span, :] = low
        d_query = d_query + jnp.where(mine, jnp.dot(low, keys, preferred_element_type=F32), 0.0)
    attended = attended.astype(BF)
    d_keys = dot(low_s[...], jnp.concatenate(query_parts, axis=0), (0, 0)).astype(BF)
    d_values = dot(probs_s[...], jnp.concatenate(grad_parts, axis=0), (0, 0)).astype(BF)
    d_query = d_query.astype(BF)
    d_hidden = dot(d_keys, project_ref[:, channels : 2 * channels], (1, 1)) + dot(
        d_values, project_ref[:, 2 * channels :], (1, 1)
    )
    send_hidden(d_hidden)
    d_hidden_l = dot(d_query, project_ref[:, :channels], (1, 1))
    project = (
        dot(hidden_l, d_query, (0, 0)),
        dot(hidden, d_keys, (0, 0)),
        dot(hidden, d_values, (0, 0)),
    )
    output = dot(attended, go, (0, 0))
    gain_sum = jnp.sum(d_hidden * scaled, axis=0, keepdims=True) + jnp.sum(
        d_hidden_l * scaled_l, axis=0, keepdims=True
    )
    folded = jnp.concatenate(bias_parts + [jnp.zeros((8 - heads, lanes), F32)], axis=0)
    bias_sum = lax.dot_general(
        folded,
        one_hot(dims, lanes),
        (((1,), (1,)), ((), ())),
        precision=lax.Precision.HIGHEST,
        preferred_element_type=F32,
    )
    return d_hidden, d_hidden_l, project, output, gain_sum, bias_sum, scaled_l, inverse_l


MESH = pl.DeviceIdType.MESH
AXES = ("gx", "gy", "gz")
TURNS = [(x, y, z) for x in (0, -1, 1) for y in (0, -1, 1) for z in (0, -1, 1)][1:]
FLAT = [turn for turn in TURNS if turn[2] == 0]
EDGES = [turn for turn in TURNS if turn[2] != 0]


def span_of(turn, size):
    return {0: (0, size), 1: (size - RADIUS, size), -1: (0, RADIUS)}[turn]


def rim_of(turn, size):
    return {
        0: (RADIUS, size + RADIUS),
        1: (size + RADIUS, size + 2 * RADIUS),
        -1: (0, RADIUS),
    }[turn]


def kernel(
    inner, dims, sizes, factor, chunk,
    tokens_hbm, gain_hbm, project_hbm, output_hbm, bias_hbm, go_hbm,
    token_out, project_out, output_out, gain_out, bias_out,
    table, probs_s, low_s, spread,
    edge_f, edge, main, rims, padded, hidden_f, pack_f, out_main, out_edge, in_main, in_edge,
    sums_f, sums, parts, final,
    tokens_ref, gain_ref, project_ref, output_ref, bias_ref, go_ref,
    tok_send, tok_recv, ret_send, ret_recv, rs_send, rs_recv, ag_send, ag_recv, in_sem,
):
    fetches = [
        pltpu.make_async_copy(source, target, in_sem.at[n])
        for n, (source, target) in enumerate((
            (tokens_hbm, tokens_ref), (bias_hbm, bias_ref), (gain_hbm, gain_ref),
            (project_hbm, project_ref), (output_hbm, output_ref), (go_hbm, go_ref),
        ))
    ]
    for fetch in fetches:
        fetch.start()
    size_x, size_y, size_z = inner
    pad_x, pad_y, pad_z = dims
    rows = size_x * size_y * size_z
    lanes, channels = padded.shape
    heads = bias_ref.shape[0]
    here = [lax.axis_index(axis) for axis in AXES]
    count = sizes[0] * sizes[1] * sizes[2]
    me = (here[0] * sizes[1] + here[1]) * sizes[2] + here[2]

    def peer(k):
        other = lax.rem(me + k, count)
        rest = lax.div(other, sizes[2])
        place = (lax.div(rest, sizes[1]), lax.rem(rest, sizes[1]), lax.rem(other, sizes[2]))
        return other, dict(zip(AXES, place))

    def exists(turn, sign):
        ok = None
        for at, size, step in zip(here, sizes, turn):
            if step:
                this = (at + sign * step >= 0) & (at + sign * step < size)
                ok = this if ok is None else ok & this
        return ok

    def neighbour(turn):
        return {axis: at + step for axis, at, step in zip(AXES, here, turn)}

    main[...] = jnp.zeros_like(main)
    rims[...] = jnp.zeros_like(rims)
    in_main[...] = jnp.zeros_like(in_main)
    in_edge[...] = jnp.zeros_like(in_edge)
    barrier = pltpu.get_barrier_semaphore()

    def greet(k, carry):
        pl.semaphore_signal(barrier, inc=1, device_id=peer(k)[1], device_id_type=MESH)
        return carry

    lax.fori_loop(1, count, greet, 0, unroll=count <= 32)
    fetches[0].wait()
    for x in range(size_x):
        for y in range(size_y):
            line = tokens_ref[x, y].astype(F32)
            at = (x * size_y + y) * RADIUS
            edge_f[0, at : at + RADIUS, :] = line[:RADIUS]
            edge_f[1, at : at + RADIUS, :] = line[size_z - RADIUS :]
    edge[...] = edge_f[...].astype(BF)
    pl.semaphore_wait(barrier, count - 1)

    def token_copy(turn):
        n = TURNS.index(turn)
        if turn[2]:
            source = edge.at[1 if turn[2] > 0 else 0]
            target = rims.at[EDGES.index(turn)]
        else:
            (x0, x1), (y0, y1) = (span_of(t, s) for t, s in zip(turn[:2], inner[:2]))
            (u0, u1), (v0, v1) = (rim_of(-t, s) for t, s in zip(turn[:2], inner[:2]))
            source = tokens_ref.at[x0:x1, y0:y1]
            target = main.at[u0:u1, v0:v1]
        return pltpu.make_async_remote_copy(
            src_ref=source, dst_ref=target, send_sem=tok_send.at[n], recv_sem=tok_recv.at[n],
            device_id=neighbour(turn), device_id_type=MESH,
        )

    def grad_copy(turn):
        n = TURNS.index(turn)
        if turn[2]:
            source, target = (buffer.at[EDGES.index(turn)] for buffer in (out_edge, in_edge))
        else:
            (u0, u1), (v0, v1) = (rim_of(t, s) for t, s in zip(turn[:2], inner[:2]))
            source = out_main.at[u0:u1, v0:v1]
            target = in_main.at[FLAT.index(turn), 0 : u1 - u0, 0 : v1 - v0]
        return pltpu.make_async_remote_copy(
            src_ref=source, dst_ref=target, send_sem=ret_send.at[n], recv_sem=ret_recv.at[n],
            device_id=neighbour(turn), device_id_type=MESH,
        )

    def every(make, sign, what):
        for turn in TURNS:
            pl.when(exists(turn, sign))(lambda turn=turn: getattr(make(turn), what)())

    every(token_copy, 1, "start")
    fetches[1].wait()
    bias_table(
        bias_ref, spread, table, inner, dims, lanes,
        [(at, size * cells) for at, size, cells in zip(here, sizes, inner)],
    )
    for fetch in fetches[2:]:
        fetch.wait()
    every(token_copy, -1, "wait_recv")

    filled = pad_x * pad_y * pad_z
    if filled < lanes:
        padded[filled:, :] = jnp.zeros((lanes - filled, channels), F32)
    sides = [
        [(t, u - rim_of(-t, s)[0] + span_of(t, s)[0]) for u in range(s + 2 * RADIUS)
         for t in (0, 1, -1) if rim_of(-t, s)[0] <= u < rim_of(-t, s)[1]]
        for s in inner[:2]
    ]
    for u in range(pad_x):
        for v in range(pad_y):
            (turn_x, x), (turn_y, y) = sides[0][u], sides[1][v]
            at = (u * pad_y + v) * pad_z
            own = turn_x == 0 and turn_y == 0
            line = tokens_ref[x, y] if own else main[u, v]
            padded[at + RADIUS : at + RADIUS + size_z, :] = line.astype(F32)
            row = (x * size_y + y) * RADIUS
            for turn_z, to in ((1, at), (-1, at + RADIUS + size_z)):
                tile = rims[EDGES.index((turn_x, turn_y, turn_z))].astype(F32)
                padded[to : to + RADIUS, :] = tile[row : row + RADIUS]

    def send_hidden(d_hidden):
        hidden_f[...] = d_hidden
        pack_f[...] = jnp.zeros_like(pack_f)
        for u in range(pad_x):
            for v in range(pad_y):
                (turn_x, x), (turn_y, y) = sides[0][u], sides[1][v]
                at = (u * pad_y + v) * pad_z
                out_main[u, v] = hidden_f[at + RADIUS : at + RADIUS + size_z, :].astype(BF)
                row = (x * size_y + y) * RADIUS
                for turn_z, to in ((-1, at), (1, at + RADIUS + size_z)):
                    slot = EDGES.index((-turn_x, -turn_y, turn_z))
                    pack_f[slot, row : row + RADIUS, :] = hidden_f[to : to + RADIUS, :]
        out_edge[...] = pack_f[...].astype(BF)
        every(grad_copy, 1, "start")

    _, d_hidden_l, project, output, gain_sum, bias_sum, scaled, inverse = attention_grads(
        padded[...], tokens_ref[...].astype(F32).reshape(rows, channels), gain_ref[...],
        project_ref, output_ref, go_ref[...], table, probs_s, low_s, inner, dims, heads,
        send_hidden,
    )
    used = 4 * channels
    blocks = project + (output,)
    full = jnp.concatenate(blocks, axis=0).astype(BF)
    if count * chunk > used:
        full = jnp.concatenate([full, jnp.zeros((count * chunk - used, channels), BF)], axis=0)
    sums[:, 0:chunk, :] = full.reshape(count, chunk, channels)
    sums_f[0:8, :] = bias_sum
    sums_f[8:16, :] = jnp.broadcast_to(gain_sum, (8, channels))
    sums[:, chunk:, :] = jnp.broadcast_to(sums_f[...].astype(BF)[None], (count, 16, channels))

    def part_copy(k):
        other, place = peer(k)
        return pltpu.make_async_remote_copy(
            src_ref=sums.at[other], dst_ref=parts.at[me], send_sem=rs_send.at[k],
            recv_sem=rs_recv.at[k], device_id=place, device_id_type=MESH,
        )

    def part_arrival(k):
        other = lax.rem(me + count - k, count)
        return pltpu.make_async_remote_copy(
            src_ref=sums.at[other], dst_ref=parts.at[other], send_sem=rs_send.at[k],
            recv_sem=rs_recv.at[k], device_id=peer(k)[1], device_id_type=MESH,
        )

    def whole_copy(k):
        place = peer(k)[1]
        return pltpu.make_async_remote_copy(
            src_ref=final.at[me], dst_ref=final.at[me], send_sem=ag_send.at[k],
            recv_sem=ag_recv.at[k], device_id=place, device_id_type=MESH,
        )

    def whole_arrival(k):
        other = lax.rem(me + count - k, count)
        return pltpu.make_async_remote_copy(
            src_ref=final.at[other], dst_ref=final.at[other], send_sem=ag_send.at[k],
            recv_sem=ag_recv.at[k], device_id=peer(k)[1], device_id_type=MESH,
        )

    def loop(body):
        lax.fori_loop(1, count, lambda k, carry: (body(k), carry)[1], 0, unroll=count <= 32)

    loop(lambda k: part_copy(k).start())
    parts[me] = sums[me]

    every(grad_copy, -1, "wait_recv")
    norm_scaled = d_hidden_l
    low = jnp.zeros(in_edge.shape[1:], F32)
    high = jnp.zeros(in_edge.shape[1:], F32)
    for n, turn in enumerate(EDGES):
        if turn[2] > 0:
            low = low + in_edge[n].astype(F32)
        else:
            high = high + in_edge[n].astype(F32)
    for x in range(size_x):
        for y in range(size_y):
            at = ((x + RADIUS) * pad_y + y + RADIUS) * pad_z + RADIUS
            line = hidden_f[at : at + size_z, :]
            for n, (turn_x, turn_y, _) in enumerate(FLAT):
                (x0, x1), (y0, y1) = span_of(-turn_x, size_x), span_of(-turn_y, size_y)
                if x0 <= x < x1 and y0 <= y < y1:
                    line = line + in_main[n, x - x0, y - y0].astype(F32)
            to = (x * size_y + y) * size_z
            row = (x * size_y + y) * RADIUS
            padded[to : to + size_z, :] = line
            padded[to : to + RADIUS, :] += low[row : row + RADIUS]
            padded[to + size_z - RADIUS : to + size_z, :] += high[row : row + RADIUS]
    d_scaled = (padded[0:rows, :] + norm_scaled) * gain_ref[...]
    token_grad = inverse * (
        d_scaled - scaled * jnp.mean(d_scaled * scaled, axis=-1, keepdims=True)
    )
    token_out[...] = token_grad.reshape(inner + (channels,))

    loop(lambda k: part_arrival(k).wait_recv())
    total = lax.fori_loop(
        1, count, lambda k, carry: carry + parts[k].astype(F32), parts[0].astype(F32)
    ) * factor
    final[me] = total[0:chunk].astype(BF)
    loop(lambda k: whole_copy(k).start())
    loop(lambda k: whole_arrival(k).wait_recv())
    done = final[...].astype(F32).reshape(count * chunk, channels)
    for i in range(3):
        project_out[:, i * channels : (i + 1) * channels] = done[i * channels : (i + 1) * channels]
    output_out[...] = done[3 * channels : used]
    bias_out[...] = total[chunk : chunk + heads, : WIN**3]
    gain_out[...] = total[chunk + 8 : chunk + 9]
    every(token_copy, 1, "wait_send")
    every(grad_copy, 1, "wait_send")
    loop(lambda k: part_copy(k).wait_send())
    loop(lambda k: whole_copy(k).wait_send())


def write_out(*refs):
    sources, targets, held, in_sem, out_sem = refs[:5], list(refs[5:10]), refs[10:15], refs[15], refs[16]
    takes = [pltpu.make_async_copy(sources[n], held[n], in_sem.at[n]) for n in range(5)]
    gives = [
        pltpu.make_async_copy(held[n].at[0] if n == 3 else held[n], targets[n], out_sem.at[n])
        for n in range(5)
    ]
    for copy in takes:
        copy.start()
    for take, give in zip(takes, gives):
        take.wait()
        give.start()
    for copy in gives:
        copy.wait()


def shards(tokens, norm_gain, project_weight, output_weight, position_bias, grad_output):
    inner, channels = tokens.shape[:3], tokens.shape[3]
    heads = position_bias.shape[0]
    sizes = tuple(lax.axis_size(axis) for axis in AXES)
    dims = tuple(size + 2 * RADIUS for size in inner)
    rows = inner[0] * inner[1] * inner[2]
    lanes = -(-dims[0] * dims[1] * dims[2] // 128) * 128
    count = sizes[0] * sizes[1] * sizes[2]
    factor = (rows * count) ** (-0.5)
    chunk = -(-4 * channels // (16 * count)) * 16
    tile = inner[0] * inner[1] * RADIUS
    vmem = pl.BlockSpec(memory_space=pltpu.VMEM)
    many = len(TURNS)
    out = pl.pallas_call(
        functools.partial(kernel, inner, dims, sizes, factor, chunk),
        out_shape=(
            jax.ShapeDtypeStruct(tokens.shape, F32),
            jax.ShapeDtypeStruct((channels, 3 * channels), F32),
            jax.ShapeDtypeStruct((channels, channels), F32),
            jax.ShapeDtypeStruct((1, channels), F32),
            jax.ShapeDtypeStruct(position_bias.shape, F32),
        ),
        in_specs=[pl.BlockSpec(memory_space=pltpu.HBM)] * 6,
        out_specs=(vmem,) * 5,
        scratch_shapes=[
            pltpu.VMEM((heads * rows, lanes), F32),
            pltpu.VMEM((heads * rows, lanes), BF),
            pltpu.VMEM((heads * rows, lanes), BF),
            pltpu.VMEM((8, 128), F32),
            pltpu.VMEM((2, tile, channels), F32),
            pltpu.VMEM((2, tile, channels), BF),
            pltpu.VMEM((dims[0], dims[1], inner[2], channels), BF),
            pltpu.VMEM((len(EDGES), tile, channels), BF),
            pltpu.VMEM((lanes, channels), F32),
            pltpu.VMEM((lanes, channels), F32),
            pltpu.VMEM((len(EDGES), tile, channels), F32),
            pltpu.VMEM((dims[0], dims[1], inner[2], channels), BF),
            pltpu.VMEM((len(EDGES), tile, channels), BF),
            pltpu.VMEM((len(FLAT),) + inner + (channels,), BF),
            pltpu.VMEM((len(EDGES), tile, channels), BF),
            pltpu.VMEM((16, channels), F32),
            pltpu.VMEM((count, chunk + 16, channels), BF),
            pltpu.VMEM((count, chunk + 16, channels), BF),
            pltpu.VMEM((count, chunk, channels), BF),
            pltpu.VMEM(tokens.shape, BF),
            pltpu.VMEM((1, channels), F32),
            pltpu.VMEM(project_weight.shape, BF),
            pltpu.VMEM(output_weight.shape, BF),
            pltpu.VMEM(position_bias.shape, F32),
            pltpu.VMEM((rows, channels), BF),
        ]
        + [pltpu.SemaphoreType.DMA((many,))] * 4
        + [pltpu.SemaphoreType.DMA((count,))] * 4
        + [pltpu.SemaphoreType.DMA((6,))],
        compiler_params=pltpu.CompilerParams(
            vmem_limit_bytes=62 * 2**20, collective_id=0, has_side_effects=True
        ),
    )(
        tokens,
        norm_gain.reshape(1, channels),
        project_weight,
        output_weight,
        position_bias,
        grad_output.reshape(rows, channels),
    )
    results = pl.pallas_call(
        write_out,
        out_shape=tuple(
            jax.ShapeDtypeStruct((channels,) if n == 3 else part.shape, F32)
            for n, part in enumerate(out)
        ),
        in_specs=[pl.BlockSpec(memory_space=pltpu.HBM)] * 5,
        out_specs=(pl.BlockSpec(memory_space=pltpu.HBM),) * 5,
        scratch_shapes=[pltpu.VMEM(part.shape, F32) for part in out]
        + [pltpu.SemaphoreType.DMA((5,))] * 2,
        compiler_params=pltpu.CompilerParams(vmem_limit_bytes=62 * 2**20),
    )(*out)
    return tuple(results)


def solution(mesh):
    tokens = P(("groups", "gx"), "gy", "gz", None)
    return jax.shard_map(
        shards,
        mesh=mesh,
        in_specs=(tokens, P(), P(), P(), P(), tokens),
        out_specs=(tokens, P("groups", None), P("groups", None), P("groups"), P("groups", None)),
        check_vma=False,
    )
```
